32 devices in a mesh: dp: 16 (over z, y, x), mp: 2 (over core).
Axes of the slice: x: 2, y: 2, z: 4, core: 2. Of those that a mesh axis runs over, the one named last changes fastest.
Arguments:
- molecules: bfloat16 [32, 512, 768], P('dp', 'mp'), may hold values from -6 to 6
- gain_attn: float32 [768], replicated, may hold values from 0.1 to 1.9
- w_query: bfloat16 [768, 768], P(None, 'mp'), may hold values from -0.21875 to 0.21875
- w_key: bfloat16 [768, 768], P(None, 'mp'), may hold values from -0.21875 to 0.21875
- w_value: bfloat16 [768, 768], P(None, 'mp'), may hold values from -0.21875 to 0.21875
- w_output: bfloat16 [768, 768], P('mp'), may hold values from -0.875 to 0.875
- gain_ffn: float32 [768], replicated, may hold values from 0.1 to 1.9
- w_inner: bfloat16 [768, 3072], P(None, 'mp'), may hold values from -0.21875 to 0.21875
- w_outer: bfloat16 [3072, 768], P('mp'), may hold values from -0.109375 to 0.109375
- cotangent: bfloat16 [32, 512, 768], P('dp', 'mp'), may hold values from -6 to 6
- span_mask: int32 [32, 512], P('dp', 'mp'), may hold values 0 or 1
Outputs:
- activations: bfloat16 [32, 512, 768], P('dp', 'mp')
- grad_molecules: float32 [32, 512, 768], P('dp', 'mp')
- grad_query: float32 [768, 768], P(None, 'mp')
- grad_key: float32 [768, 768], P(None, 'mp')
- grad_value: float32 [768, 768], P(None, 'mp')
- grad_output: float32 [768, 768], P('mp')
- grad_inner: float32 [768, 3072], P(None, 'mp')
- grad_outer: float32 [3072, 768], P('mp')
- grad_gain_attn: float32 [768], replicated
- grad_gain_ffn: float32 [768], replicated
The draws below stay inside these ranges and needn't reach their ends.
All inputs are finite; a program needn't handle non-finite values. No bound on the sum of `span_mask` on one device may be relied on, other than what follows from the above.
Results may differ from the reference program's by a relative error of at most 0.013.
Values may be sent and summed in bfloat16 or wider, within the bound.
A program may use at most 128 MiB of HBM per device.

```python
import jax
import jax.numpy as jnp
from jax import lax

D = 768
HEADS = 12
HEAD_DIM = 64
FF = 3072
LENGTH = 512
SEQS = 32


def touch_ends(drawn, rng, smallest, top_value):
    longest = drawn.shape.index(max(drawn.shape))
    spots = []
    for shift in (0, 1):
        where = [jax.random.randint(jax.random.fold_in(rng, axis), (), 0, length) for axis, length in enumerate(drawn.shape)]
        where[longest] = (where[longest] + shift) % drawn.shape[longest]
        spots.append(tuple(where))
    return drawn.at[spots[0]].set(smallest).at[spots[1]].set(top_value)


def level_of(own_key, dims, shards, least, largest):
    def one(position, shards_of):
        draws = jax.random.uniform(jax.random.fold_in(jax.random.fold_in(own_key, 6), position), (shards_of,), jnp.float32, least / len(shards), largest / len(shards))
        return jnp.repeat(jnp.exp(draws), dims[position] // shards_of).reshape((-1,) + (1,) * (len(dims) - position - 1))

    loudness = one(*shards[0])
    for cut in shards[1:]:
        loudness = loudness * one(*cut)
    return loudness


def bell_draw(stream_key, shape, deviation, most, pieces=(), kind=jnp.bfloat16):
    level = level_of(stream_key, shape, pieces, -0.22, 0.18) if pieces else 1.0
    entries = jax.random.normal(stream_key, shape, jnp.float32) * deviation * level
    return jnp.minimum(jnp.maximum(entries, -most), most).astype(kind)


def setup_inputs(seed: int = 0) -> dict:
    key_list = jax.random.split(jax.random.key(seed), 12)
    return {
        "molecules": bell_draw(key_list[0], (SEQS, LENGTH, D), 1.0, 6.0, ((0, 16), (1, 2))),
        "gain_attn": jnp.clip(1.0 + 0.18 * jax.random.normal(key_list[1], (D,), jnp.float32), 0.1, 1.9),
        "w_query": bell_draw(key_list[2], (D, D), D ** -0.5, 0.21875, ((1, 2),)),
        "w_key": bell_draw(key_list[3], (D, D), D ** -0.5, 0.21875, ((1, 2),)),
        "w_value": bell_draw(key_list[4], (D, D), D ** -0.5, 0.21875, ((1, 2),)),
        "w_output": bell_draw(key_list[5], (D, D), (D // 16) ** -0.5, 0.875, ((0, 2),)),
        "gain_ffn": jnp.clip(1.0 + 0.18 * jax.random.normal(key_list[6], (D,), jnp.float32), 0.1, 1.9),
        "w_inner": bell_draw(key_list[7], (D, FF), D ** -0.5, 0.21875, ((1, 2),)),
        "w_outer": bell_draw(key_list[8], (FF, D), FF ** -0.5, 0.109375, ((0, 2),)),
        "cotangent": bell_draw(key_list[9], (SEQS, LENGTH, D), 1.0, 6.0, ((0, 16), (1, 2))),
        "span_mask": touch_ends((jax.random.randint(key_list[10], (SEQS, LENGTH), 0, 20) < 3).astype(jnp.int32), jax.random.fold_in(key_list[10], 1), 0, 1),
    }


EPSILON = 1e-05

@jax.custom_vjp
def low(v):
    return lax.optimization_barrier(v.astype(jnp.bfloat16)).astype(jnp.float32)

@jax.custom_vjp
def low_back(v):
    return v

def low_keep(v):
    return (low(v), None)

def low_pass(kept, grad):
    return (grad,)

def back_keep(v):
    return (v, None)

def back_low(kept, grad):
    return (low(grad),)
low.defvjp(low_keep, low_pass)
low_back.defvjp(back_keep, back_low)

def product(left_side, right_side):
    return jnp.dot(left_side, right_side, precision=lax.Precision.HIGHEST)

def normalize(values, gain):
    centred = values - lax.optimization_barrier(jnp.mean(values, axis=-1, keepdims=True))
    variance = lax.optimization_barrier(jnp.mean(centred * centred, axis=-1, keepdims=True))
    return centred * lax.rsqrt(variance + EPSILON) * gain

def block_forward(inputs, gain_attn, w_query, w_key, w_value, w_output, gain_ffn, w_inner, w_outer):
    length = inputs.shape[0]
    normed_one = low(normalize(inputs, gain_attn))

    def project(weight):
        return low_back(low(product(normed_one, weight))).reshape(length, HEADS, HEAD_DIM)
    queries = project(w_query)
    keys_all = project(w_key)
    values_all = project(w_value)
    scores = jnp.einsum('qhd,khd->hqk', queries, keys_all, precision=lax.Precision.HIGHEST)
    scores = low_back(scores * HEAD_DIM ** (-0.5))
    probs = low(jax.nn.softmax(scores, axis=-1))
    mixed = jnp.einsum('hqk,khd->qhd', probs, values_all, precision=lax.Precision.HIGHEST)
    mixed = low_back(low(mixed.reshape(length, HEADS * HEAD_DIM)))
    hidden = inputs + low_back(product(mixed, w_output))
    normed_two = low(normalize(hidden, gain_ffn))
    inner = low_back(product(normed_two, w_inner))
    active = low(jax.nn.gelu(inner, approximate=False))
    return hidden + low_back(product(active, w_outer))

def reference(molecules, gain_attn, w_query, w_key, w_value, w_output, gain_ffn, w_inner, w_outer, cotangent, span_mask):
    params = tuple((weight.astype(jnp.float32) for weight in (gain_attn, w_query, w_key, w_value, w_output, gain_ffn, w_inner, w_outer)))

    def per_sequence(running, sequence):
        inputs, grad_seed, masked = sequence
        result, pullback = jax.vjp(block_forward, inputs.astype(jnp.float32), *params)
        loss_weight = 0.25 + 0.75 * masked.astype(jnp.float32)
        gradients = pullback(grad_seed.astype(jnp.float32) * loss_weight[:, None])
        running = jax.tree.map(jnp.add, running, tuple(gradients[1:]))
        return (running, (result.astype(jnp.bfloat16), gradients[0]))
    initial = tuple((jnp.zeros_like(weight) for weight in params))
    totals, (outputs, input_grads) = lax.scan(per_sequence, initial, (molecules, cotangent, span_mask))
    grad_gain_attn, grad_query, grad_key, grad_value, grad_output, grad_gain_ffn, grad_inner, grad_outer = totals
    return (outputs, input_grads, grad_query, grad_key, grad_value, grad_output, grad_inner, grad_outer, grad_gain_attn, grad_gain_ffn)
```

```python
import jax
import jax.numpy as jnp
import functools
from jax import lax
from jax.experimental import pallas as pl
from jax.experimental.pallas import tpu as pltpu
from jax.sharding import PartitionSpec as P

HEAD_DIM = 64


EPSILON = 1e-05


def normalize(values, gain):
    centred = values - jnp.mean(values, axis=-1, keepdims=True)
    inv_std = lax.rsqrt(jnp.mean(centred * centred, axis=-1, keepdims=True) + EPSILON)
    scaled = centred * inv_std
    return (scaled * gain, scaled, inv_std)


def norm_back(grad_normed, scaled, inv_std, gain):
    grad_scaled = grad_normed * gain
    mean_first = jnp.mean(grad_scaled, axis=-1, keepdims=True)
    mean_second = jnp.mean(grad_scaled * scaled, axis=-1, keepdims=True)
    grad_values = inv_std * (grad_scaled - mean_first - scaled * mean_second)
    return (grad_values, jnp.sum(grad_normed * scaled, axis=0))


def gelu_exact(values):
    return jax.nn.gelu(values, approximate=False)


def product_rows(pairs):
    summed = None
    for left_side, right_side, flipped in pairs:
        contract = ((1,), (1,)) if flipped else ((1,), (0,))
        partial_term = lax.dot_general(
            left_side, right_side, (contract, ((), ())), preferred_element_type=jnp.float32
        )
        summed = partial_term if summed is None else summed + partial_term
    return summed


def forward_sum(pairs):
    return lax.psum_scatter(product_rows(pairs), "mp", scatter_dimension=0, tiled=True)


def backward_sum(pairs):
    return lax.psum_scatter(product_rows(pairs), "mp", scatter_dimension=0, tiled=True)


def rows_gather(values):
    return lax.all_gather(values, "mp", axis=0, tiled=True)


def grads_gather(values):
    return lax.all_gather(values, "mp", axis=0, tiled=True)


def weight_grad(left_side, right_side):
    return lax.dot_general(
        left_side, right_side, (((0,), (0,)), ((), ())), preferred_element_type=jnp.float32
    )


def times_transposed(left_side, right_side):
    return lax.dot_general(
        left_side, right_side, (((1,), (1,)), ((), ())), preferred_element_type=jnp.float32
    )


MESH = pl.DeviceIdType.MESH
ROWS = 1536
HALF = ROWS // 2
QUAD = HALF // 2
CHUNK = QUAD // 4
PART = CHUNK // 2
bf16 = jnp.bfloat16
f32 = jnp.float32


def al(v, m):
    return pl.multiple_of(v, m)


class Ring:
    def __init__(self, grads, far, up, down, near, beyond, whole, out, sems, dp_size):
        self.grads, self.far, self.up, self.down, self.near, self.beyond, self.whole, self.out = (
            grads, far, up, down, near, beyond, whole, out)
        self.send_sem, self.recv_sem, self.own_sem = sems
        self.dp = lax.axis_index("dp")
        self.mp = lax.axis_index("mp")
        self.place = lax.rem(lax.div(self.dp, 4), 4)
        bits = (lax.rem(self.dp, 2), lax.rem(lax.div(self.dp, 2), 2))
        self.first_bit = bits
        self.last_bit = (bits[1], bits[0])
        self.extra = (dp_size // 16).bit_length() - 1

    def kept(self, h):
        return h * HALF + self.first_bit[h] * QUAD

    def chunk(self, h, q, n=1):
        return pl.ds(al(self.kept(h) + q * CHUNK, 16), n * CHUNK)

    def copy(self, src, dst, u, h, which, dp):
        return pltpu.make_async_remote_copy(
            src_ref=src, dst_ref=dst, send_sem=self.send_sem.at[u, h, which],
            recv_sem=self.recv_sem.at[u, h, which], device_id=(dp, self.mp), device_id_type=MESH)

    def first_peer(self, h):
        return self.dp + (1 - 2 * self.first_bit[h]) * (1 << h)

    def last_peer(self, h):
        return self.dp + (1 - 2 * self.last_bit[h]) * (1 << (1 - h))

    def c_first(self, u, h):
        rows = pl.ds(al(h * HALF + (1 - self.first_bit[h]) * QUAD, 16), QUAD)
        return self.copy(self.grads.at[u, rows], self.far.at[u, h], u, h, 0, self.first_peer(h))

    def c_up(self, u, h, q, n):
        return self.copy(self.grads.at[u, self.chunk(h, q, n)], self.up.at[u, h, pl.ds(q * CHUNK, n * CHUNK)],
                         u, h, 1, self.dp + 4)

    def c_down(self, u, h, q, n):
        return self.copy(self.grads.at[u, self.chunk(h, q, n)], self.down.at[u, h, pl.ds(q * CHUNK, n * CHUNK)],
                         u, h, 2, self.dp - 4)

    def part(self, h, side):
        return pl.ds(al(self.kept(h) + self.place * CHUNK + side * PART, 16), PART)

    def c_last(self, u, h):
        return self.copy(self.grads.at[u, self.part(h, 1 - self.last_bit[h])], self.near.at[u, h],
                         u, h, 3, self.last_peer(h))

    def whole_part(self, h):
        return pl.ds(al(self.place * CHUNK + self.last_bit[h] * PART, 16), PART)

    def c_last_back(self, u, h):
        block = self.whole.at[u, h, self.whole_part(h)]
        return self.copy(block, block, u, h, 4, self.last_peer(h))

    def c_gather(self, u, h, q, step, upward):
        block = self.whole.at[u, h, pl.ds(q * CHUNK, CHUNK)]
        return self.copy(block, block, u, h,
                         (5 if upward else 8) + step, self.dp + 4 if upward else self.dp - 4)

    def c_first_back(self, u, h):
        rows = pl.ds(al(self.kept(h), 16), QUAD)
        return self.copy(self.whole.at[u, h], self.out.at[u, rows], u, h, 11, self.first_peer(h))

    def c_own(self, u, h):
        rows = pl.ds(al(self.kept(h), 16), QUAD)
        return pltpu.make_async_copy(self.whole.at[u, h], self.out.at[u, rows], self.own_sem.at[u, h])

    def add(self, u, rows, other):
        self.grads[u, rows] = (self.grads[u, rows].astype(f32) + other.astype(f32)).astype(bf16)

    def at_place(self, p, fn):
        pl.when(self.place == p)(fn)

    def stage0(self, u):
        for h in range(2):
            self.c_first(u, h).start()

    def stage1(self, u):
        for h in range(2):
            c = self.c_first(u, h)
            c.wait_recv()
            self.add(u, pl.ds(al(self.kept(h), 16), QUAD), self.far[u, h])

            def low():
                self.c_up(u, h, 1, 3).start()

            def high():
                self.c_down(u, h, 0, 3).start()
            self.at_place(0, low)
            self.at_place(3, high)

    def stage2(self, u):
        for h in range(2):
            def low():
                self.c_up(u, h, 1, 3).wait_recv()
                self.add(u, self.chunk(h, 1, 3), self.up[u, h, pl.ds(CHUNK, 3 * CHUNK)])
                self.c_up(u, h, 2, 2).start()

            def high():
                self.c_down(u, h, 0, 3).wait_recv()
                self.add(u, self.chunk(h, 0, 3), self.down[u, h, pl.ds(0, 3 * CHUNK)])
                self.c_down(u, h, 0, 2).start()
            self.at_place(1, low)
            self.at_place(2, high)

    def stage3(self, u):
        for h in range(2):
            def low():
                self.c_down(u, h, 0, 2).wait_recv()
                self.add(u, self.chunk(h, 0, 2), self.down[u, h, pl.ds(0, 2 * CHUNK)])
                self.c_down(u, h, 0, 1).start()
                self.c_last(u, h).start()

            def high():
                self.c_up(u, h, 2, 2).wait_recv()
                self.add(u, self.chunk(h, 2, 2), self.up[u, h, pl.ds(2 * CHUNK, 2 * CHUNK)])
                self.c_up(u, h, 3, 1).start()
                self.c_last(u, h).start()
            self.at_place(1, low)
            self.at_place(2, high)

    def stage4(self, u):
        for h in range(2):
            def low():
                self.c_down(u, h, 0, 1).wait_recv()
                self.add(u, self.chunk(h, 0), self.down[u, h, pl.ds(0, CHUNK)])
                self.c_last(u, h).start()

            def high():
                self.c_up(u, h, 3, 1).wait_recv()
                self.add(u, self.chunk(h, 3), self.up[u, h, pl.ds(3 * CHUNK, CHUNK)])
                self.c_last(u, h).start()
            self.at_place(0, low)
            self.at_place(3, high)

    def stage5(self, u):
        for h in range(2):
            self.c_last(u, h).wait_recv()
            mine = self.part(h, self.last_bit[h])
            if self.extra:
                self.add(u, mine, self.near[u, h])
            for k in range(self.extra):
                c = self.copy(self.grads.at[u, mine], self.beyond.at[u, h, k], u, h, 12 + k, self.dp ^ (16 << k))
                c.start()
                c.wait()
                if k < self.extra - 1:
                    self.add(u, mine, self.beyond[u, h, k])
            last = self.beyond[u, h, self.extra - 1] if self.extra else self.near[u, h]
            self.whole[u, h, self.whole_part(h)] = (self.grads[u, mine].astype(f32) + last.astype(f32)).astype(bf16)
            self.c_last_back(u, h).start()

    def stage6(self, u):
        for h in range(2):
            self.c_last_back(u, h).wait_recv()
            for p in range(4):
                def go(p=p):
                    if p < 3:
                        self.c_gather(u, h, p, 0, True).start()
                    if p > 0:
                        self.c_gather(u, h, p, 0, False).start()
                self.at_place(p, go)

    def stage_gather(self, u, step):
        for h in range(2):
            for p in range(4):
                def go(p=p):
                    if p - step >= 0:
                        self.c_gather(u, h, p - step, step - 1, True).wait_recv()
                        if p < 3 and step < 3:
                            self.c_gather(u, h, p - step, step, True).start()
                    if p + step <= 3:
                        self.c_gather(u, h, p + step, step - 1, False).wait_recv()
                        if p > 0 and step < 3:
                            self.c_gather(u, h, p + step, step, False).start()
                self.at_place(p, go)
            if step == 3:
                self.c_first_back(u, h).start()
                self.c_own(u, h).start()

    def stage10(self, u):
        for h in range(2):
            self.c_first_back(u, h).wait_recv()

    def stage_sent(self, u):
        for h in range(2):
            self.c_first(u, h).wait_send()
            self.c_last(u, h).wait_send()
            self.c_last_back(u, h).wait_send()
            self.c_first_back(u, h).wait_send()
            self.c_own(u, h).wait()
            for p in range(4):
                def go(p=p):
                    if p < 3:
                        self.c_up(u, h, p + 1, 3 - p).wait_send()
                    if p > 0:
                        self.c_down(u, h, 0, p).wait_send()
                    for step in range(3):
                        if p < 3 and p - step >= 0:
                            self.c_gather(u, h, p - step, step, True).wait_send()
                        if p > 0 and p + step <= 3:
                            self.c_gather(u, h, p + step, step, False).wait_send()
                self.at_place(p, go)

    def stages(self):
        return [self.stage0, self.stage1, self.stage2, self.stage3, self.stage4, self.stage5, self.stage6,
                lambda u: self.stage_gather(u, 1), lambda u: self.stage_gather(u, 2), lambda u: self.stage_gather(u, 3),
                self.stage10]

    def barrier(self):
        bar = pltpu.get_barrier_semaphore()
        peers = [1, 2, 4, 12] + [16 << k for k in range(self.extra)]
        for flip in peers:
            pl.semaphore_signal(bar, inc=1, device_id=(self.dp ^ flip, self.mp), device_id_type=MESH)
        pl.semaphore_wait(bar, len(peers))


def scratch(units, dp_size):
    extra = (dp_size // 16).bit_length() - 1
    return [
        pltpu.VMEM((units, 2, QUAD, 128), bf16),
        pltpu.VMEM((units, 2, QUAD, 128), bf16),
        pltpu.VMEM((units, 2, QUAD, 128), bf16),
        pltpu.VMEM((units, 2, PART, 128), bf16),
        pltpu.VMEM((units, 2, max(extra, 1), PART, 128), bf16),
        pltpu.VMEM((units, 2, QUAD, 128), bf16),
        pltpu.SemaphoreType.DMA((units, 2, 12 + extra)),
        pltpu.SemaphoreType.DMA((units, 2, 12 + extra)),
        pltpu.SemaphoreType.DMA((units, 2)),
    ]


def kernel(units, lags, dp_size, g_in, g_out, grads, far, up, down, near, beyond, whole, ssem, rsem, osem, lsem):
    ring = Ring(grads, far, up, down, near, beyond, whole, g_out, (ssem, rsem, osem), dp_size)
    def load(u):
        return pltpu.make_async_copy(g_in.at[u], grads.at[u], lsem.at[u])
    def start_load(u, c):
        load(u).start()
        return c
    lax.fori_loop(0, units, start_load, 0)
    ring.barrier()
    stages = ring.stages()

    def tick(t, c):
        for s in range(len(stages) - 1, -1, -1):
            u = t - lags[s]

            @pl.when((u >= 0) & (u < units))
            def _():
                if s == 0:
                    load(u).wait()
                stages[s](u)
        return c
    lax.fori_loop(0, units + lags[-1], tick, 0)

    def finish(u, c):
        ring.stage_sent(u)
        return c
    lax.fori_loop(0, units, finish, 0)


def all_sum(g, dp_size, lags, cid=0, name="grad_sum"):
    units = g.shape[0]
    return pl.pallas_call(
        functools.partial(kernel, units, lags, dp_size),
        out_shape=jax.ShapeDtypeStruct(g.shape, bf16),
        in_specs=[pl.BlockSpec(memory_space=pl.ANY)],
        out_specs=pl.BlockSpec(memory_space=pl.ANY),
        scratch_shapes=[pltpu.VMEM((units, ROWS, 128), bf16)] + scratch(units, dp_size)
        + [pltpu.SemaphoreType.DMA((units,))],
        compiler_params=pltpu.CompilerParams(collective_id=cid, has_side_effects=True, vmem_limit_bytes=56 * 2**20),
        name=name,
    )(g)


def pack(values):
    rows, columns = values.shape
    return values.astype(bf16).reshape(rows, columns // 128, 128).transpose(1, 0, 2).reshape(-1, 128)


def unpack(packed, rows, columns):
    return packed.reshape(columns // 128, rows, 128).transpose(1, 0, 2).reshape(rows, columns).astype(f32)


def sum_weights(parts):
    packed = jnp.concatenate([pack(part) for part in parts])
    summed = all_sum(packed.reshape(-1, ROWS, 128), lax.axis_size("dp"), [0, 3, 4, 5, 6, 7, 8, 9, 10, 11, 14])
    summed = summed.reshape(-1, 128)
    outs, at = [], 0
    for part in parts:
        count = part.size // 128
        outs.append(unpack(summed[at : at + count], *part.shape))
        at += count
    return outs


def per_device(
    molecules,
    gain_attn,
    w_query,
    w_key,
    w_value,
    w_output,
    gain_ffn,
    w_inner,
    w_outer,
    cotangent,
    span_mask,
):
    batches, shard_rows, width = molecules.shape
    local_heads = w_query.shape[1] // HEAD_DIM
    scale_factor = HEAD_DIM ** (-0.5)
    acc_query = jnp.zeros(w_query.shape, jnp.float32)
    acc_key = jnp.zeros(w_key.shape, jnp.float32)
    acc_value = jnp.zeros(w_value.shape, jnp.float32)
    acc_output = jnp.zeros(w_output.shape, jnp.float32)
    acc_inner = jnp.zeros(w_inner.shape, jnp.float32)
    acc_outer = jnp.zeros(w_outer.shape, jnp.float32)
    gain_one_acc = jnp.zeros((width,), jnp.float32)
    gain_two_acc = jnp.zeros((width,), jnp.float32)
    results = []
    input_grads = []
    for micro_batch in range(batches):
        inputs = molecules[micro_batch].astype(jnp.float32)
        normed_one, scaled_one, inv_one = normalize(inputs, gain_attn)
        full_one = rows_gather(normed_one.astype(jnp.bfloat16))
        length = full_one.shape[0]
        queries = jnp.dot(full_one, w_query, preferred_element_type=jnp.float32).astype(
            jnp.bfloat16
        )
        keys_all = jnp.dot(full_one, w_key, preferred_element_type=jnp.float32).astype(jnp.bfloat16)
        values_all = jnp.dot(full_one, w_value, preferred_element_type=jnp.float32).astype(
            jnp.bfloat16
        )
        head_q = queries.reshape(length, local_heads, HEAD_DIM)
        head_k = keys_all.reshape(length, local_heads, HEAD_DIM)
        head_v = values_all.reshape(length, local_heads, HEAD_DIM)
        scores = (
            jnp.einsum("qhd,khd->hqk", head_q, head_k, preferred_element_type=jnp.float32)
            * scale_factor
        )
        row_max = jnp.max(scores, axis=-1, keepdims=True)
        expon = jnp.exp(scores - row_max)
        row_total = jnp.sum(expon, axis=-1, keepdims=True)
        log_total = row_max + jnp.log(row_total)
        probs_low = (expon / row_total).astype(jnp.bfloat16)
        mixed = jnp.einsum("hqk,khd->qhd", probs_low, head_v, preferred_element_type=jnp.float32)
        mixed = mixed.reshape(length, local_heads * HEAD_DIM).astype(jnp.bfloat16)
        hidden = inputs + forward_sum(((mixed, w_output, False),))
        normed_two, scaled_two, inv_two = normalize(hidden, gain_ffn)
        full_two = rows_gather(normed_two.astype(jnp.bfloat16))
        inner = jnp.dot(full_two, w_inner, preferred_element_type=jnp.float32)
        active = gelu_exact(inner).astype(jnp.bfloat16)
        result = hidden + forward_sum(((active, w_outer, False),))
        results.append(result.astype(jnp.bfloat16))
        loss_weight = 0.25 + 0.75 * span_mask[micro_batch].astype(jnp.float32)
        grad_result = cotangent[micro_batch].astype(jnp.float32) * loss_weight[:, None]
        grad_full = grads_gather(grad_result.astype(jnp.bfloat16))
        acc_outer = acc_outer + weight_grad(active, grad_full)
        grad_active = times_transposed(grad_full, w_outer)
        gelu_value, gelu_pull = jax.vjp(gelu_exact, inner)
        grad_inner = gelu_pull(grad_active)[0].astype(jnp.bfloat16)
        acc_inner = acc_inner + weight_grad(full_two, grad_inner)
        grad_normed_two = backward_sum(((grad_inner, w_inner, True),))
        grad_hidden_norm, gain_part = norm_back(grad_normed_two, scaled_two, inv_two, gain_ffn)
        gain_two_acc = gain_two_acc + gain_part
        grad_hidden = grad_result + grad_hidden_norm
        grad_branch = grads_gather(grad_hidden.astype(jnp.bfloat16))
        acc_output = acc_output + weight_grad(mixed, grad_branch)
        grad_mixed = times_transposed(grad_branch, w_output).astype(jnp.bfloat16)
        grad_mixed = grad_mixed.reshape(length, local_heads, HEAD_DIM)
        scores_again = (
            jnp.einsum("qhd,khd->hqk", head_q, head_k, preferred_element_type=jnp.float32)
            * scale_factor
        )
        probs_again = jnp.exp(scores_again - log_total)
        grad_values = jnp.einsum(
            "hqk,qhd->khd",
            probs_again.astype(jnp.bfloat16),
            grad_mixed,
            preferred_element_type=jnp.float32,
        )
        grad_values = grad_values.reshape(length, local_heads * HEAD_DIM).astype(jnp.bfloat16)
        grad_probs = jnp.einsum(
            "qhd,khd->hqk", grad_mixed, head_v, preferred_element_type=jnp.float32
        )
        row_inner = jnp.sum(grad_probs * probs_again, axis=-1, keepdims=True)
        grad_scores = (probs_again * (grad_probs - row_inner)).astype(jnp.bfloat16)
        grad_queries = (
            jnp.einsum("hqk,khd->qhd", grad_scores, head_k, preferred_element_type=jnp.float32)
            * scale_factor
        )
        grad_queries = grad_queries.reshape(length, local_heads * HEAD_DIM).astype(jnp.bfloat16)
        grad_keys = (
            jnp.einsum("hqk,qhd->khd", grad_scores, head_q, preferred_element_type=jnp.float32)
            * scale_factor
        )
        grad_keys = grad_keys.reshape(length, local_heads * HEAD_DIM).astype(jnp.bfloat16)
        acc_query = acc_query + weight_grad(full_one, grad_queries)
        acc_key = acc_key + weight_grad(full_one, grad_keys)
        acc_value = acc_value + weight_grad(full_one, grad_values)
        grad_normed_one = backward_sum(
            ((grad_queries, w_query, True), (grad_keys, w_key, True), (grad_values, w_value, True))
        )
        grad_input_norm, gain_part = norm_back(grad_normed_one, scaled_one, inv_one, gain_attn)
        gain_one_acc = gain_one_acc + gain_part
        input_grads.append(grad_hidden + grad_input_norm)
    acc_query, acc_key, acc_value, acc_output, acc_inner, acc_outer = sum_weights(
        (acc_query, acc_key, acc_value, acc_output, acc_inner, acc_outer)
    )
    gain_one_acc, gain_two_acc = lax.psum((gain_one_acc, gain_two_acc), ("dp", "mp"))
    return (
        jnp.stack(results),
        jnp.stack(input_grads),
        acc_query,
        acc_key,
        acc_value,
        acc_output,
        acc_inner,
        acc_outer,
        gain_one_acc,
        gain_two_acc,
    )


def solution(mesh):
    in_specs = (
        P("dp", "mp", None),
        P(),
        P(None, "mp"),
        P(None, "mp"),
        P(None, "mp"),
        P("mp", None),
        P(),
        P(None, "mp"),
        P("mp", None),
        P("dp", "mp", None),
        P("dp", "mp"),
    )
    out_specs = (
        P("dp", "mp", None),
        P("dp", "mp", None),
        P(None, "mp"),
        P(None, "mp"),
        P(None, "mp"),
        P("mp", None),
        P(None, "mp"),
        P("mp", None),
        P(),
        P(),
    )
    return jax.shard_map(
        per_device, mesh=mesh, in_specs=in_specs, out_specs=out_specs, check_vma=False
    )
```

```python
import functools

import jax
import jax.numpy as jnp
from jax import lax
from jax.experimental import pallas as pl
from jax.experimental.pallas import tpu as pltpu
from jax.sharding import PartitionSpec as P

HEAD_DIM = 64
EPSILON = 1e-05
MESH = pl.DeviceIdType.MESH
bf16 = jnp.bfloat16
f32 = jnp.float32

ROWS = 1536
HALF = ROWS // 2
QUAD = HALF // 2
CHUNK = QUAD // 4
PART = CHUNK // 2


def al(v, m):
    return pl.multiple_of(v, m)


class Ring:
    def __init__(self, grads, far, up, down, near, beyond, whole, out, sems, dp_size):
        self.grads, self.far, self.up, self.down, self.near, self.beyond, self.whole, self.out = (
            grads, far, up, down, near, beyond, whole, out)
        self.send_sem, self.recv_sem, self.own_sem = sems
        self.dp = lax.axis_index("dp")
        self.mp = lax.axis_index("mp")
        self.place = lax.rem(lax.div(self.dp, 4), 4)
        bits = (lax.rem(self.dp, 2), lax.rem(lax.div(self.dp, 2), 2))
        self.first_bit = bits
        self.last_bit = (bits[1], bits[0])
        self.extra = (dp_size // 16).bit_length() - 1

    def kept(self, h):
        return h * HALF + self.first_bit[h] * QUAD

    def chunk(self, h, q, n=1):
        return pl.ds(al(self.kept(h) + q * CHUNK, 16), n * CHUNK)

    def copy(self, src, dst, u, h, which, dp):
        return pltpu.make_async_remote_copy(
            src_ref=src, dst_ref=dst, send_sem=self.send_sem.at[u, h, which],
            recv_sem=self.recv_sem.at[u, h, which], device_id=(dp, self.mp), device_id_type=MESH)

    def first_peer(self, h):
        return self.dp + (1 - 2 * self.first_bit[h]) * (1 << h)

    def last_peer(self, h):
        return self.dp + (1 - 2 * self.last_bit[h]) * (1 << (1 - h))

    def c_first(self, u, h):
        rows = pl.ds(al(h * HALF + (1 - self.first_bit[h]) * QUAD, 16), QUAD)
        return self.copy(self.grads.at[u, rows], self.far.at[u, h], u, h, 0, self.first_peer(h))

    def c_up(self, u, h, q, n):
        return self.copy(self.grads.at[u, self.chunk(h, q, n)], self.up.at[u, h, pl.ds(q * CHUNK, n * CHUNK)],
                         u, h, 1, self.dp + 4)

    def c_down(self, u, h, q, n):
        return self.copy(self.grads.at[u, self.chunk(h, q, n)], self.down.at[u, h, pl.ds(q * CHUNK, n * CHUNK)],
                         u, h, 2, self.dp - 4)

    def part(self, h, side):
        return pl.ds(al(self.kept(h) + self.place * CHUNK + side * PART, 16), PART)

    def c_last(self, u, h):
        return self.copy(self.grads.at[u, self.part(h, 1 - self.last_bit[h])], self.near.at[u, h],
                         u, h, 3, self.last_peer(h))

    def whole_part(self, h):
        return pl.ds(al(self.place * CHUNK + self.last_bit[h] * PART, 16), PART)

    def c_last_back(self, u, h):
        block = self.whole.at[u, h, self.whole_part(h)]
        return self.copy(block, block, u, h, 4, self.last_peer(h))

    def c_gather(self, u, h, q, step, upward):
        block = self.whole.at[u, h, pl.ds(q * CHUNK, CHUNK)]
        return self.copy(block, block, u, h,
                         (5 if upward else 8) + step, self.dp + 4 if upward else self.dp - 4)

    def c_first_back(self, u, h):
        rows = pl.ds(al(self.kept(h), 16), QUAD)
        return self.copy(self.whole.at[u, h], self.out.at[u, rows], u, h, 11, self.first_peer(h))

    def c_own(self, u, h):
        rows = pl.ds(al(self.kept(h), 16), QUAD)
        return pltpu.make_async_copy(self.whole.at[u, h], self.out.at[u, rows], self.own_sem.at[u, h])

    def add(self, u, rows, other):
        self.grads[u, rows] = (self.grads[u, rows].astype(f32) + other.astype(f32)).astype(bf16)

    def at_place(self, p, fn):
        pl.when(self.place == p)(fn)

    def stage0(self, u):
        for h in range(2):
            self.c_first(u, h).start()

    def stage1(self, u):
        for h in range(2):
            c = self.c_first(u, h)
            c.wait_recv()
            self.add(u, pl.ds(al(self.kept(h), 16), QUAD), self.far[u, h])

            def low():
                self.c_up(u, h, 1, 3).start()

            def high():
                self.c_down(u, h, 0, 3).start()
            self.at_place(0, low)
            self.at_place(3, high)

    def stage2(self, u):
        for h in range(2):
            def low():
                self.c_up(u, h, 1, 3).wait_recv()
                self.add(u, self.chunk(h, 1, 3), self.up[u, h, pl.ds(CHUNK, 3 * CHUNK)])
                self.c_up(u, h, 2, 2).start()

            def high():
                self.c_down(u, h, 0, 3).wait_recv()
                self.add(u, self.chunk(h, 0, 3), self.down[u, h, pl.ds(0, 3 * CHUNK)])
                self.c_down(u, h, 0, 2).start()
            self.at_place(1, low)
            self.at_place(2, high)

    def stage3(self, u):
        for h in range(2):
            def low():
                self.c_down(u, h, 0, 2).wait_recv()
                self.add(u, self.chunk(h, 0, 2), self.down[u, h, pl.ds(0, 2 * CHUNK)])
                self.c_down(u, h, 0, 1).start()
                self.c_last(u, h).start()

            def high():
                self.c_up(u, h, 2, 2).wait_recv()
                self.add(u, self.chunk(h, 2, 2), self.up[u, h, pl.ds(2 * CHUNK, 2 * CHUNK)])
                self.c_up(u, h, 3, 1).start()
                self.c_last(u, h).start()
            self.at_place(1, low)
            self.at_place(2, high)

    def stage4(self, u):
        for h in range(2):
            def low():
                self.c_down(u, h, 0, 1).wait_recv()
                self.add(u, self.chunk(h, 0), self.down[u, h, pl.ds(0, CHUNK)])
                self.c_last(u, h).start()

            def high():
                self.c_up(u, h, 3, 1).wait_recv()
                self.add(u, self.chunk(h, 3), self.up[u, h, pl.ds(3 * CHUNK, CHUNK)])
                self.c_last(u, h).start()
            self.at_place(0, low)
            self.at_place(3, high)

    def stage5(self, u):
        for h in range(2):
            self.c_last(u, h).wait_recv()
            mine = self.part(h, self.last_bit[h])
            if self.extra:
                self.add(u, mine, self.near[u, h])
            for k in range(self.extra):
                c = self.copy(self.grads.at[u, mine], self.beyond.at[u, h, k], u, h, 12 + k, self.dp ^ (16 << k))
                c.start()
                c.wait()
                if k < self.extra - 1:
                    self.add(u, mine, self.beyond[u, h, k])
            last = self.beyond[u, h, self.extra - 1] if self.extra else self.near[u, h]
            self.whole[u, h, self.whole_part(h)] = (self.grads[u, mine].astype(f32) + last.astype(f32)).astype(bf16)
            self.c_last_back(u, h).start()

    def stage6(self, u):
        for h in range(2):
            self.c_last_back(u, h).wait_recv()
            for p in range(4):
                def go(p=p):
                    if p < 3:
                        self.c_gather(u, h, p, 0, True).start()
                    if p > 0:
                        self.c_gather(u, h, p, 0, False).start()
                self.at_place(p, go)

    def stage_gather(self, u, step):
        for h in range(2):
            for p in range(4):
                def go(p=p):
                    if p - step >= 0:
                        self.c_gather(u, h, p - step, step - 1, True).wait_recv()
                        if p < 3 and step < 3:
                            self.c_gather(u, h, p - step, step, True).start()
                    if p + step <= 3:
                        self.c_gather(u, h, p + step, step - 1, False).wait_recv()
                        if p > 0 and step < 3:
                            self.c_gather(u, h, p + step, step, False).start()
                self.at_place(p, go)
            if step == 3:
                self.c_first_back(u, h).start()
                self.c_own(u, h).start()

    def stage10(self, u):
        for h in range(2):
            self.c_first_back(u, h).wait_recv()

    def stage_sent(self, u):
        for h in range(2):
            self.c_first(u, h).wait_send()
            self.c_last(u, h).wait_send()
            self.c_last_back(u, h).wait_send()
            self.c_first_back(u, h).wait_send()
            self.c_own(u, h).wait()
            for p in range(4):
                def go(p=p):
                    if p < 3:
                        self.c_up(u, h, p + 1, 3 - p).wait_send()
                    if p > 0:
                        self.c_down(u, h, 0, p).wait_send()
                    for step in range(3):
                        if p < 3 and p - step >= 0:
                            self.c_gather(u, h, p - step, step, True).wait_send()
                        if p > 0 and p + step <= 3:
                            self.c_gather(u, h, p + step, step, False).wait_send()
                self.at_place(p, go)

    def stages(self):
        return [self.stage0, self.stage1, self.stage2, self.stage3, self.stage4, self.stage5, self.stage6,
                lambda u: self.stage_gather(u, 1), lambda u: self.stage_gather(u, 2), lambda u: self.stage_gather(u, 3),
                self.stage10]

    def barrier(self):
        bar = pltpu.get_barrier_semaphore()
        peers = [1, 2, 4, 12] + [16 << k for k in range(self.extra)]
        for flip in peers:
            pl.semaphore_signal(bar, inc=1, device_id=(self.dp ^ flip, self.mp), device_id_type=MESH)
        pl.semaphore_wait(bar, len(peers))


def scratch(units, dp_size):
    extra = (dp_size // 16).bit_length() - 1
    return [
        pltpu.VMEM((units, 2, QUAD, 128), bf16),
        pltpu.VMEM((units, 2, QUAD, 128), bf16),
        pltpu.VMEM((units, 2, QUAD, 128), bf16),
        pltpu.VMEM((units, 2, PART, 128), bf16),
        pltpu.VMEM((units, 2, max(extra, 1), PART, 128), bf16),
        pltpu.SemaphoreType.DMA((units, 2, 12 + extra)),
        pltpu.SemaphoreType.DMA((units, 2, 12 + extra)),
        pltpu.SemaphoreType.DMA((units, 2)),
    ]


def dot(a, b):
    return jnp.dot(a, b, preferred_element_type=f32)


def dot_nt(a, b):
    return lax.dot_general(a, b, (((1,), (1,)), ((), ())), preferred_element_type=f32)


def dot_tn(a, b):
    return lax.dot_general(a, b, (((0,), (0,)), ((), ())), preferred_element_type=f32)


def normalize(values):
    centred = values - jnp.mean(values, axis=-1, keepdims=True)
    inv_std = lax.rsqrt(jnp.mean(centred * centred, axis=-1, keepdims=True) + EPSILON)
    return centred * inv_std, inv_std


def norm_back(grad, scaled, inv_std, gain):
    grad_scaled = grad * gain
    mean_first = jnp.mean(grad_scaled, axis=-1, keepdims=True)
    mean_second = jnp.mean(grad_scaled * scaled, axis=-1, keepdims=True)
    return inv_std * (grad_scaled - mean_first - scaled * mean_second), jnp.sum(grad * scaled, axis=0, keepdims=True)


FF_UNITS = 12
UNITS = 18
GAP = 8
LAGS = (0, 3, 4, 5, 6, 7, 8, 9, 10, 11, 14)
BLOCK = 256


def layer_kernel(
    dp_size, mol_hbm, gain_one, wq_hbm, wk_hbm, wv_hbm, wo_hbm, gain_two, wi_hbm, wu_hbm, cot_hbm, mask_ref,
    act_hbm, gmol_hbm, sums_hbm, gains_hbm,
    x, cot, wqkv, wo, wi, wu, n1, turned, qkv, mixed, mixed_t, hid, pin, pout, n2, gres, act, gip, gbr, lse,
    gains_sum, gains_in, grads, far, up, down, near, beyond,
    in_sem, out_sem, mp_send, mp_recv, gain_send, gain_recv, ring_send, ring_recv, ring_own,
):
    mp = lax.axis_index("mp")
    dp = lax.axis_index("dp")
    length = n1.shape[0] // 2
    own_rows = length // 2
    width = n1.shape[1]
    heads_width = wo.shape[0]
    pairs = heads_width // 128
    ring = Ring(grads, far, up, down, near, beyond, far, sums_hbm, (ring_send, ring_recv, ring_own), dp_size)
    stages = ring.stages()

    def own(s):
        return pl.ds(al(s * length + mp * own_rows, own_rows), own_rows)

    def other(s):
        return pl.ds(al(s * length + (1 - mp) * own_rows, own_rows), own_rows)

    def seq(s):
        return pl.ds(s * length, length)

    def to_peer(src, dst, k):
        return pltpu.make_async_remote_copy(
            src_ref=src, dst_ref=dst, send_sem=mp_send.at[k], recv_sem=mp_recv.at[k],
            device_id=(dp, 1 - mp), device_id_type=MESH)

    def rows_copy(ref, s, k):
        return to_peer(ref.at[own(s)], ref.at[own(s)], k)

    def part_copy(kind, s):
        return to_peer(pout.at[kind, s], pin.at[kind, s], 8 + 2 * kind + s)

    def tick(t):
        for k in range(len(stages) - 1, -1, -1):
            v = t - LAGS[k]
            late = v >= FF_UNITS
            u = jnp.where(late, v - GAP, v)
            if isinstance(t, int):
                if v < 0 or FF_UNITS <= v < FF_UNITS + GAP or v >= UNITS + GAP:
                    continue
                stages[k](v if v < FF_UNITS else v - GAP)
            else:
                live = ((v >= 0) & (v < FF_UNITS)) | ((v >= FF_UNITS + GAP) & (v < UNITS + GAP))
                pl.when(live)(functools.partial(stages[k], u))

    loads = [
        pltpu.make_async_copy(mol_hbm.at[0], x.at[0], in_sem.at[0]),
        pltpu.make_async_copy(mol_hbm.at[1], x.at[1], in_sem.at[1]),
        pltpu.make_async_copy(wq_hbm, wqkv.at[:, pl.ds(0, heads_width)], in_sem.at[2]),
        pltpu.make_async_copy(wk_hbm, wqkv.at[:, pl.ds(heads_width, heads_width)], in_sem.at[3]),
        pltpu.make_async_copy(wv_hbm, wqkv.at[:, pl.ds(2 * heads_width, heads_width)], in_sem.at[4]),
        pltpu.make_async_copy(cot_hbm, cot, in_sem.at[5]),
        pltpu.make_async_copy(wo_hbm, wo, in_sem.at[6]),
        pltpu.make_async_copy(wi_hbm, wi, in_sem.at[7]),
        pltpu.make_async_copy(wu_hbm, wu, in_sem.at[8]),
    ]
    for load in loads:
        load.start()

    barrier = pltpu.get_barrier_semaphore()
    flips = [1, 2, 4, 8, 12] + [16 << k for k in range(ring.extra)]
    for flip in flips:
        pl.semaphore_signal(barrier, inc=1, device_id=(dp ^ flip, mp), device_id_type=MESH)
    pl.semaphore_signal(barrier, inc=1, device_id=(dp, 1 - mp), device_id_type=MESH)

    with jax.named_scope("norm_one"):
        for s in range(2):
            loads[s].wait()
            scaled, _ = normalize(x[s].astype(f32))
            n1[own(s), :] = (scaled * gain_one[...]).astype(bf16)
            if s == 0:
                pl.semaphore_wait(barrier, len(flips) + 1)
            rows_copy(n1, s, s).start()

    with jax.named_scope("grad_result"):
        loads[5].wait()
        lanes = lax.broadcasted_iota(jnp.int32, (128, 128), 1)
        subs = lax.broadcasted_iota(jnp.int32, (128, 128), 0)
        for s in range(2):
            for piece in range(own_rows // 128):
                row = mask_ref[pl.ds(s, 1), pl.ds(piece * 128, 128)].astype(f32)
                column = jnp.sum(jnp.where(lanes == subs, row, 0.0), axis=1, keepdims=True)
                weight = 0.25 + 0.75 * column
                values = cot[s, pl.ds(piece * 128, 128), :].astype(f32) * weight
                gres[pl.ds(al(s * length + mp * own_rows + piece * 128, 128), 128), :] = values.astype(bf16)
            rows_copy(gres, s, 2 + s).start()

    lane = lax.broadcasted_iota(jnp.int32, (1, 128), 1)
    sides = (lane < HEAD_DIM, lane >= HEAD_DIM)
    scale = HEAD_DIM ** -0.5

    with jax.named_scope("attention"):
        for load in loads[2:5]:
            load.wait()
        loads[6].wait()
        for s in range(2):
            rows_copy(n1, s, s).wait_recv()
            qkv[seq(s), :] = dot(n1[seq(s), :], wqkv[...]).astype(bf16)
            logs = jnp.zeros((length, 128), f32)
            for pair in range(pairs):
                query = qkv[seq(s), pl.ds(pair * 128, 128)] * jnp.asarray(scale, bf16)
                key = qkv[seq(s), pl.ds(heads_width + pair * 128, 128)]
                value = qkv[seq(s), pl.ds(2 * heads_width + pair * 128, 128)]
                outs = []
                for side in range(2):
                    scores = dot_nt(jnp.where(sides[side], query, 0), key)
                    row_max = jnp.max(scores, axis=-1, keepdims=True)
                    expon = jnp.exp(scores - row_max)
                    total = jnp.sum(expon, axis=-1, keepdims=True)
                    logs = jnp.where(lane == 2 * pair + side, row_max + jnp.log(total), logs)
                    outs.append(dot(expon.astype(bf16), value) * (1.0 / total))
                mixed[seq(s), pl.ds(pair * 128, 128)] = jnp.where(sides[0], outs[0], outs[1]).astype(bf16)
            lse[s] = logs
            pout[0, s] = dot(mixed[other(s), :], wo[...]).astype(bf16)
            part_copy(0, s).start()
            hid[s] = x[s].astype(f32) + dot(mixed[own(s), :], wo[...])

    with jax.named_scope("norm_two"):
        for s in range(2):
            part_copy(0, s).wait_recv()
            hidden = hid[s] + pin[0, s].astype(f32)
            hid[s] = hidden
            scaled, _ = normalize(hidden)
            n2[own(s), :] = (scaled * gain_two[...]).astype(bf16)
            rows_copy(n2, s, 4 + s).start()
        for s in range(2):
            rows_copy(gres, s, 2 + s).wait_recv()
        loads[7].wait()
        loads[8].wait()
        for s in range(2):
            rows_copy(n2, s, 4 + s).wait_recv()
        turned[...] = n2[...].T

    def feed_forward(b, carry):
        columns = pl.ds(al(b * BLOCK, BLOCK), BLOCK)
        with jax.named_scope("grad_outer"):
            inner = dot(n2[...], wi[:, columns])
            shape = 1.0 + lax.erf(inner * (0.5 ** 0.5))
            active = (0.5 * inner * shape).astype(bf16)
            act[:, columns] = active
            slope = 0.5 * shape + inner * (jnp.exp(-0.5 * inner * inner) * (2.0 * 3.141592653589793) ** -0.5)
            part = dot(active.T, gres[...]).astype(bf16)
            for g in range(width // 128):
                grads[2 * b, pl.ds(g * BLOCK, BLOCK), :] = part[:, g * 128:(g + 1) * 128]
        tick(2 * b)
        with jax.named_scope("grad_inner"):
            back = dot_nt(gres[...], wu[columns, :])
            pre = (back * slope).astype(bf16)
            gip[:, columns] = pre
            part = dot(turned[...], pre).astype(bf16)
            for g in range(BLOCK // 128):
                grads[2 * b + 1, pl.ds(g * width, width), :] = part[:, g * 128:(g + 1) * 128]
        tick(2 * b + 1)
        return carry
    lax.fori_loop(0, wi.shape[1] // BLOCK, feed_forward, 0)

    with jax.named_scope("branch_two"):
        for s in range(2):
            pout[1, s] = dot_nt(gip[other(s), :], wi[...]).astype(bf16)
            part_copy(1, s).start()
        for s in range(2):
            pout[2, s] = dot(act[other(s), :], wu[...]).astype(bf16)
            part_copy(2, s).start()
        tick(12)
        gain_two_sum = jnp.zeros((1, width), f32)
        for s in range(2):
            result = hid[s] + dot(act[own(s), :], wu[...])
            part_copy(2, s).wait_recv()
            cot[s] = (result + pin[2, s].astype(f32)).astype(bf16)
            pltpu.make_async_copy(cot.at[s], act_hbm.at[s], out_sem.at[s]).start()
            grad = dot_nt(gip[own(s), :], wi[...])
            part_copy(1, s).wait_recv()
            scaled, inv_std = normalize(hid[s])
            grad_values, gain_part = norm_back(grad + pin[1, s].astype(f32), scaled, inv_std, gain_two[...])
            gain_two_sum += gain_part
            grad_hidden = gres[own(s), :].astype(f32) + grad_values
            hid[s] = grad_hidden
            gbr[own(s), :] = grad_hidden.astype(bf16)
            rows_copy(gbr, s, 6 + s).start()
        mixed_t[...] = mixed[...].T
        turned[...] = n1[...].T
        tick(13)

    with jax.named_scope("grad_output"):
        for s in range(2):
            rows_copy(gbr, s, 6 + s).wait_recv()
            mixed[seq(s), :] = dot_nt(gbr[seq(s), :], wo[...]).astype(bf16)
        part = dot(mixed_t[...], gbr[...]).astype(bf16)
        for g in range(width // 128):
            at = g * heads_width
            grads[FF_UNITS + at // ROWS, pl.ds(at % ROWS, heads_width), :] = part[:, g * 128:(g + 1) * 128]

    def attention_back(s, pair):
        rows = pl.ds(al(s * length, length), length)

        def columns(kind):
            return pl.ds(al(kind * heads_width + pair * 128, 128), 128)
        query = qkv[rows, columns(0)] * jnp.asarray(scale, bf16)
        key = qkv[rows, columns(1)]
        value = qkv[rows, columns(2)]
        grad_mixed = mixed[rows, columns(0)]
        logs = lse[s]
        found = []
        for side in range(2):
            log_total = jnp.sum(jnp.where(lane == 2 * pair + side, logs, 0.0), axis=-1, keepdims=True)
            probs = jnp.exp(dot_nt(jnp.where(sides[side], query, 0), key) - log_total)
            grad_probs = dot_nt(jnp.where(sides[side], grad_mixed, 0), value)
            row_inner = jnp.sum(probs * grad_probs, axis=-1, keepdims=True)
            grad_scores = (probs * (grad_probs - row_inner)).astype(bf16)
            grad_value = dot_tn(probs.astype(bf16), grad_mixed)
            grad_query = dot(grad_scores, key) * scale
            grad_key = dot_tn(grad_scores, query)
            found.append((grad_query, grad_key, grad_value))
        for kind in range(3):
            act[rows, columns(kind)] = jnp.where(sides[0], found[0][kind], found[1][kind]).astype(bf16)
        tick(FF_UNITS + 2 + s * pairs + pair)
    with jax.named_scope("attention_back"):
        for s in range(2):
            for pair in range(pairs):
                attention_back(s, pair)

    with jax.named_scope("grad_projections"):
        at = FF_UNITS * ROWS + width * heads_width // 128
        for kind in range(3):
            part = dot(turned[...], act[:, pl.ds(kind * heads_width, heads_width)]).astype(bf16)
            for g in range(pairs):
                grads[at // ROWS, pl.ds(at % ROWS, width), :] = part[:, g * 128:(g + 1) * 128]
                at += width

    first = FF_UNITS + GAP
    with jax.named_scope("grad_molecules"):
        tick(first)
        joined = 3 * heads_width
        for s in range(2):
            pout[3, s] = dot_nt(act[other(s), pl.ds(0, joined)], wqkv[...]).astype(bf16)
            part_copy(3, s).start()
        gain_one_sum = jnp.zeros((1, width), f32)
        for s in range(2):
            grad = dot_nt(act[own(s), pl.ds(0, joined)], wqkv[...])
            part_copy(3, s).wait_recv()
            scaled, inv_std = normalize(x[s].astype(f32))
            grad_values, gain_part = norm_back(grad + pin[3, s].astype(f32), scaled, inv_std, gain_one[...])
            gain_one_sum += gain_part
            hid[s] = hid[s] + grad_values
            pltpu.make_async_copy(hid.at[s], gmol_hbm.at[s], out_sem.at[2 + s]).start()
        gains_sum[0] = jnp.zeros(gains_sum.shape[1:], f32)
        for g in range(width // 128):
            gains_sum[0, pl.ds(g, 1), :] = gain_one_sum[:, g * 128:(g + 1) * 128]
            gains_sum[0, pl.ds(8 + g, 1), :] = gain_two_sum[:, g * 128:(g + 1) * 128]

    targets = [(dp, 1 - mp)] + [(dp ^ (1 << k), mp) for k in range(4 + ring.extra)]

    def gain_copy(k):
        return pltpu.make_async_remote_copy(
            src_ref=gains_sum.at[k], dst_ref=gains_in.at[k], send_sem=gain_send.at[k], recv_sem=gain_recv.at[k],
            device_id=targets[k], device_id_type=MESH)

    last_tick = UNITS + GAP + LAGS[-1]

    def drain(t, carry):
        for k in range(len(targets)):
            @pl.when(t == first + 1 + k)
            def _():
                if k:
                    gain_copy(k - 1).wait_recv()
                    gains_sum[k] = gains_sum[k - 1] + gains_in[k - 1]
                gain_copy(k).start()
        tick(t)
        return carry
    with jax.named_scope("sums"):
        lax.fori_loop(first + 1, last_tick, drain, 0)
        count = len(targets)
        gain_copy(count - 1).wait_recv()
        gains_sum[count] = gains_sum[count - 1] + gains_in[count - 1]
        gains_out = pltpu.make_async_copy(gains_sum.at[count], gains_hbm, out_sem.at[4])
        gains_out.start()

    with jax.named_scope("sent"):
        for s in range(2):
            rows_copy(n1, s, s).wait_send()
            rows_copy(gres, s, 2 + s).wait_send()
            rows_copy(n2, s, 4 + s).wait_send()
            rows_copy(gbr, s, 6 + s).wait_send()
            for kind in range(4):
                part_copy(kind, s).wait_send()
            pltpu.make_async_copy(cot.at[s], act_hbm.at[s], out_sem.at[s]).wait()
            pltpu.make_async_copy(hid.at[s], gmol_hbm.at[s], out_sem.at[2 + s]).wait()
        for k in range(count):
            gain_copy(k).wait_send()

        def sent(u, carry):
            ring.stage_sent(u)
            return carry
        lax.fori_loop(0, UNITS, sent, 0)
        gains_out.wait()


def finish_kernel(
    act_in, gmol_in, sums_in, gains_in, act_out, gmol_out, gq, gk, gv, go, gi, gu, gains_out,
    packed, query, key, value, output, inner, outer, load_sem, out_sem,
):
    width, heads_width = query.shape
    plain = [
        pltpu.make_async_copy(act_in, act_out, out_sem.at[0]),
        pltpu.make_async_copy(gmol_in, gmol_out, out_sem.at[1]),
        pltpu.make_async_copy(gains_in, gains_out, out_sem.at[2]),
    ]
    loads = [pltpu.make_async_copy(sums_in.at[u], packed.at[u], load_sem.at[u]) for u in range(UNITS)]
    for load in loads:
        load.start()
    for copy in plain:
        copy.start()
    outs = []

    def send(src, dst):
        copy = pltpu.make_async_copy(src, dst, out_sem.at[3 + len(outs)])
        copy.start()
        outs.append(copy)
    for b in range(FF_UNITS // 2):
        loads[2 * b].wait()
        for g in range(width // 128):
            outer[pl.ds(b * BLOCK, BLOCK), pl.ds(g * 128, 128)] = packed[2 * b, pl.ds(g * BLOCK, BLOCK), :].astype(f32)
        send(outer.at[pl.ds(b * BLOCK, BLOCK)], gu.at[pl.ds(b * BLOCK, BLOCK)])
        loads[2 * b + 1].wait()
        for g in range(BLOCK // 128):
            inner[:, pl.ds(b * BLOCK + g * 128, 128)] = packed[2 * b + 1, pl.ds(g * width, width), :].astype(f32)
        send(inner.at[:, pl.ds(b * BLOCK, BLOCK)], gi.at[:, pl.ds(b * BLOCK, BLOCK)])
    for u in range(FF_UNITS, UNITS):
        loads[u].wait()
    at = FF_UNITS * ROWS
    for block, target in ((output, go), (query, gq), (key, gk), (value, gv)):
        rows = block.shape[0]
        for g in range(block.shape[1] // 128):
            block[:, pl.ds(g * 128, 128)] = packed[at // ROWS, pl.ds(at % ROWS, rows), :].astype(f32)
            at += rows
        send(block, target)
    for copy in plain + outs:
        copy.wait()


ANY = pl.BlockSpec(memory_space=pl.ANY)
WHOLE = pl.BlockSpec(memory_space=pltpu.VMEM)


def per_device(
    dp_size, molecules, gain_attn, w_query, w_key, w_value, w_output, gain_ffn, w_inner, w_outer, cotangent, span_mask
):
    count, shard, width = molecules.shape
    heads_width = w_query.shape[1]
    units_inner = w_inner.shape[1]
    rows = 2 * count * shard
    extra = (dp_size // 16).bit_length() - 1
    levels = 5 + extra
    sums_shape = jax.ShapeDtypeStruct((UNITS, ROWS, 128), bf16)
    gains_shape = jax.ShapeDtypeStruct((16, 128), f32)
    mol_shape = jax.ShapeDtypeStruct(molecules.shape, f32)
    act_shape = jax.ShapeDtypeStruct(molecules.shape, bf16)
    act, gmol, sums, gains = pl.pallas_call(
        functools.partial(layer_kernel, dp_size),
        out_shape=(act_shape, mol_shape, sums_shape, gains_shape),
        in_specs=[ANY, WHOLE, ANY, ANY, ANY, ANY, WHOLE, ANY, ANY, ANY, WHOLE],
        out_specs=(ANY, ANY, ANY, ANY),
        scratch_shapes=[
            pltpu.VMEM(molecules.shape, bf16),
            pltpu.VMEM(molecules.shape, bf16),
            pltpu.VMEM((width, 3 * heads_width), bf16),
            pltpu.VMEM(w_output.shape, bf16),
            pltpu.VMEM(w_inner.shape, bf16),
            pltpu.VMEM(w_outer.shape, bf16),
            pltpu.VMEM((rows, width), bf16),
            pltpu.VMEM((width, rows), bf16),
            pltpu.VMEM((rows, 3 * heads_width), bf16),
            pltpu.VMEM((rows, heads_width), bf16),
            pltpu.VMEM((heads_width, rows), bf16),
            pltpu.VMEM(molecules.shape, f32),
            pltpu.VMEM((4,) + molecules.shape, bf16),
            pltpu.VMEM((4,) + molecules.shape, bf16),
            pltpu.VMEM((rows, width), bf16),
            pltpu.VMEM((rows, width), bf16),
            pltpu.VMEM((rows, units_inner), bf16),
            pltpu.VMEM((rows, units_inner), bf16),
            pltpu.VMEM((rows, width), bf16),
            pltpu.VMEM((count, rows // 2, 128), f32),
            pltpu.VMEM((levels + 1, 16, 128), f32),
            pltpu.VMEM((levels, 16, 128), f32),
            pltpu.VMEM((UNITS, ROWS, 128), bf16),
            pltpu.VMEM((UNITS, 2, QUAD, 128), bf16),
            pltpu.VMEM((UNITS, 2, QUAD, 128), bf16),
            pltpu.VMEM((UNITS, 2, QUAD, 128), bf16),
            pltpu.VMEM((UNITS, 2, PART, 128), bf16),
            pltpu.VMEM((UNITS, 2, max(extra, 1), PART, 128), bf16),
            pltpu.SemaphoreType.DMA((9,)),
            pltpu.SemaphoreType.DMA((5,)),
            pltpu.SemaphoreType.DMA((16,)),
            pltpu.SemaphoreType.DMA((16,)),
            pltpu.SemaphoreType.DMA((levels,)),
            pltpu.SemaphoreType.DMA((levels,)),
            pltpu.SemaphoreType.DMA((UNITS, 2, 12 + extra)),
            pltpu.SemaphoreType.DMA((UNITS, 2, 12 + extra)),
            pltpu.SemaphoreType.DMA((UNITS, 2)),
        ],
        compiler_params=pltpu.CompilerParams(
            collective_id=0, has_side_effects=True, vmem_limit_bytes=62 * 2 ** 20),
        name="layer",
    )(
        molecules, gain_attn.reshape(1, -1), w_query, w_key, w_value, w_output, gain_ffn.reshape(1, -1),
        w_inner, w_outer, cotangent, span_mask,
    )
    shapes = [jax.ShapeDtypeStruct(w.shape, f32) for w in (w_query, w_key, w_value, w_output, w_inner, w_outer)]
    outs = pl.pallas_call(
        finish_kernel,
        out_shape=(act_shape, mol_shape, *shapes, gains_shape),
        in_specs=[ANY] * 4,
        out_specs=(ANY,) * 9,
        scratch_shapes=[pltpu.VMEM((UNITS, ROWS, 128), bf16)]
        + [pltpu.VMEM(shape.shape, f32) for shape in shapes]
        + [pltpu.SemaphoreType.DMA((UNITS,)), pltpu.SemaphoreType.DMA((3 + FF_UNITS + 4,))],
        compiler_params=pltpu.CompilerParams(vmem_limit_bytes=40 * 2 ** 20),
        name="finish",
    )(act, gmol, sums, gains)
    gains = outs[-1]
    return (*outs[:-1], gains[0:6].reshape(width), gains[8:14].reshape(width))


def solution(mesh):
    in_specs = (
        P("dp", "mp", None),
        P(),
        P(None, "mp"),
        P(None, "mp"),
        P(None, "mp"),
        P("mp", None),
        P(),
        P(None, "mp"),
        P("mp", None),
        P("dp", "mp", None),
        P("dp", "mp"),
    )
    out_specs = (
        P("dp", "mp", None),
        P("dp", "mp", None),
        P(None, "mp"),
        P(None, "mp"),
        P(None, "mp"),
        P("mp", None),
        P(None, "mp"),
        P("mp", None),
        P(),
        P(),
    )
    return jax.shard_map(
        functools.partial(per_device, mesh.shape["dp"]),
        mesh=mesh, in_specs=in_specs, out_specs=out_specs, check_vma=False,
    )
```

```python
import functools

import jax
import jax.numpy as jnp
from jax import lax
from jax.experimental import pallas as pl
from jax.experimental.pallas import tpu as pltpu
from jax.sharding import PartitionSpec as P

HEAD_DIM = 64
EPSILON = 1e-05
MESH = pl.DeviceIdType.MESH
bf16 = jnp.bfloat16
f32 = jnp.float32

ROWS = 3072
HALF = ROWS // 2
QUAD = HALF // 2
SIDE = QUAD // 2
PART = SIDE // 2
FF_UNITS = 6
UNITS = 9
BLOCK = 256


VMEM_LIMIT = 54 * 2 ** 20

SCHEDULE = (
    (),
    ((0, 0),),
    (),
    ((0, 1),),
    (),
    ((0, 2),),
    ((1, 0),),
    ((0, 3),),
    (),
    ((1, 1), (0, 4),),
    (),
    ((2, 0), (1, 2), (0, 5),),
    (),
    ((2, 1),),
    ((1, 3),),
    ((3, 0),),
    ((2, 2), (1, 4),),
    (),
    ((3, 1), (2, 3),),
    ((4, 0), (1, 5),),
    ((3, 2), (0, 6),),
    ((5, 0), (2, 4),),
    ((4, 1), (3, 3),),
    ((2, 5), (0, 7),),
    ((6, 0), (4, 2), (1, 6),),
    ((5, 1), (3, 4),),
    ((4, 3), (0, 8),),
    (),
    ((3, 5), (5, 2), (7, 0), (1, 7),),
    ((6, 1), (5, 3),),
    ((4, 4), (2, 6), (1, 8), (4, 5), (6, 2), (6, 3), (5, 4), (5, 5), (8, 0), (6, 4), (9, 0), (6, 5), (2, 7),
     (3, 6), (7, 1), (3, 7), (2, 8), (8, 1), (7, 2), (4, 6), (10, 0), (5, 6), (4, 7), (6, 6), (5, 7), (9, 1),
     (3, 8), (6, 7), (7, 3), (4, 8), (10, 1), (5, 8), (8, 2), (9, 2), (7, 4), (6, 8), (8, 3), (7, 5), (9, 3),
     (10, 2), (8, 4), (7, 6), (9, 4), (10, 3), (8, 5), (7, 7), (9, 5), (10, 4), (8, 6), (7, 8), (9, 6), (10, 5),
     (8, 7), (9, 7), (10, 6), (8, 8), (9, 8), (10, 7), (10, 8),),
)


def al(v, m):
    return pl.multiple_of(v, m)


class Ring:
    def __init__(self, grads, far, line, near, beyond, out, send_sem, recv_sem, own_sem, dp_size):
        self.grads, self.far, self.line, self.near, self.beyond, self.out = grads, far, line, near, beyond, out
        self.send_sem, self.recv_sem, self.own_sem = send_sem, recv_sem, own_sem
        self.extra = (dp_size // 16).bit_length() - 1
        self.dp = lax.axis_index("dp")
        self.mp = lax.axis_index("mp")
        place = lax.rem(lax.div(self.dp, 4), 4)
        low = jnp.where(place < 2, 1, 0)
        self.is_end = (place == 0) | (place == 3)
        self.is_mid = (place == 1) | (place == 2)
        self.inward = self.dp + 4 * (2 * low - 1)
        self.outward = self.dp - 4 * (2 * low - 1)
        self.far_side = low * SIDE
        self.own_side = (1 - low) * SIDE
        bits = (lax.rem(self.dp, 2), lax.rem(lax.div(self.dp, 2), 2))
        self.first_bit = bits
        self.last_bit = (bits[1], bits[0])
        self.first_peer = [self.dp + (1 - 2 * bits[h]) * (1 << h) for h in range(2)]
        self.last_peer = [self.first_peer[1], self.first_peer[0]]

    def kept(self, h, offset, count):
        return pl.ds(al(h * HALF + self.first_bit[h] * QUAD + offset, 16), count)

    def side(self, offset, count=SIDE):
        return pl.ds(al(offset, 16), count)

    def copy(self, src, dst, u, sent, received, dp):
        return pltpu.make_async_remote_copy(
            src_ref=src, dst_ref=dst, send_sem=self.send_sem.at[u, sent], recv_sem=self.recv_sem.at[u, received],
            device_id=(dp, self.mp), device_id_type=MESH)

    def received(self, block, u, k):
        self.copy(block, block, u, k, k, self.first_peer[0]).wait_recv()

    def was_sent(self, block, u, k):
        self.copy(block, block, u, k, k, self.first_peer[0]).wait_send()

    def add(self, u, rows, other):
        self.grads[u, rows] = (self.grads[u, rows].astype(f32) + other.astype(f32)).astype(bf16)

    def pass_sum(self, u, offset, sent, received, dp):
        for h in range(2):
            self.copy(self.grads.at[u, self.kept(h, offset, SIDE)], self.line.at[u, h, self.side(offset)],
                      u, sent, received, dp).start()

    def take_sum(self, u, offset, received):
        self.received(self.line.at[u, :, self.side(offset)], u, received)
        for h in range(2):
            self.add(u, self.kept(h, offset, SIDE), self.line[u, h, self.side(offset)])

    def pass_whole(self, u, offset, sent, received, dp):
        for h in range(2):
            block = self.far.at[u, h, self.side(offset)]
            self.copy(block, block, u, sent, received, dp).start()

    def take_whole(self, u, offset, received):
        self.received(self.far.at[u, :, self.side(offset)], u, received)

    def finish(self, u):
        for h in range(2):
            rows = self.kept(h, 0, QUAD)
            self.copy(self.far.at[u, h], self.out.at[u, rows], u, 5, 5, self.first_peer[h]).start()
            pltpu.make_async_copy(self.far.at[u, h], self.out.at[u, rows], self.own_sem.at[u]).start()

    def stage0(self, u):
        for h in range(2):
            rows = pl.ds(al(h * HALF + (1 - self.first_bit[h]) * QUAD, 16), QUAD)
            self.copy(self.grads.at[u, rows], self.far.at[u, h], u, 0, 0, self.first_peer[h]).start()

    def stage1(self, u):
        self.received(self.far.at[u], u, 0)
        for h in range(2):
            self.add(u, self.kept(h, 0, QUAD), self.far[u, h])

        @pl.when(self.is_end)
        def _():
            self.pass_sum(u, self.far_side, 1, 1, self.inward)

    def stage2(self, u):
        @pl.when(self.is_mid)
        def _():
            self.take_sum(u, self.far_side, 1)
            self.pass_sum(u, self.far_side, 1, 2, self.inward)

    def stage3(self, u):
        @pl.when(self.is_mid)
        def _():
            self.take_sum(u, self.own_side, 2)
            self.pass_sum(u, self.own_side, 2, 2, self.outward)

    def stage4(self, u):
        @pl.when(self.is_end)
        def _():
            self.take_sum(u, self.own_side, 2)
            for h in range(2):
                rows = self.kept(h, self.own_side + (1 - self.last_bit[h]) * PART, PART)
                self.copy(self.grads.at[u, rows], self.near.at[u, h], u, 2, 1, self.last_peer[h]).start()

    def stage5(self, u):
        @pl.when(self.is_end)
        def _():
            self.received(self.near.at[u], u, 1)
            for h in range(2):
                offset = self.own_side + self.last_bit[h] * PART
                mine = self.kept(h, offset, PART)
                last = self.near[u, h]
                for k in range(self.extra):
                    self.add(u, mine, last)
                    copy = self.copy(self.grads.at[u, mine], self.beyond.at[u, h, k], u, 6 + 2 * k + h, 6 + 2 * k + h,
                                     self.dp ^ (16 << k))
                    copy.start()
                    copy.wait()
                    last = self.beyond[u, h, k]
                rows = self.side(offset, PART)
                self.far[u, h, rows] = (self.grads[u, mine].astype(f32) + last.astype(f32)).astype(bf16)
                block = self.far.at[u, h, rows]
                self.copy(block, block, u, 3, 3, self.last_peer[h]).start()

    def stage6(self, u):
        @pl.when(self.is_end)
        def _():
            self.received(self.near.at[u], u, 3)
            self.pass_whole(u, self.own_side, 4, 3, self.inward)

    def stage7(self, u):
        @pl.when(self.is_mid)
        def _():
            self.take_whole(u, self.own_side, 3)
            self.pass_whole(u, self.own_side, 3, 4, self.inward)

    def stage8(self, u):
        @pl.when(self.is_mid)
        def _():
            self.take_whole(u, self.far_side, 4)
            self.pass_whole(u, self.far_side, 4, 4, self.outward)
            self.finish(u)

    def stage9(self, u):
        @pl.when(self.is_end)
        def _():
            self.take_whole(u, self.far_side, 4)
            self.finish(u)

    def stage10(self, u):
        self.received(self.far.at[u], u, 5)

    def sent(self, u):
        self.was_sent(self.far.at[u], u, 0)
        self.was_sent(self.far.at[u], u, 5)
        pltpu.make_async_copy(self.far.at[u], self.far.at[u], self.own_sem.at[u]).wait()
        one_side = self.line.at[u, :, pl.ds(0, SIDE)]

        @pl.when(self.is_end)
        def _():
            for k, block in ((1, one_side), (2, self.near.at[u]), (3, self.near.at[u]), (4, one_side)):
                self.was_sent(block, u, k)

        @pl.when(self.is_mid)
        def _():
            for k in range(1, 5):
                self.was_sent(one_side, u, k)

    def stages(self):
        return (self.stage0, self.stage1, self.stage2, self.stage3, self.stage4, self.stage5, self.stage6,
                self.stage7, self.stage8, self.stage9, self.stage10)


def dot(a, b):
    return jnp.dot(a, b, preferred_element_type=f32)


def dot_nt(a, b):
    return lax.dot_general(a, b, (((1,), (1,)), ((), ())), preferred_element_type=f32)


def dot_tn(a, b):
    return lax.dot_general(a, b, (((0,), (0,)), ((), ())), preferred_element_type=f32)


def normalize(values):
    centred = values - jnp.mean(values, axis=-1, keepdims=True)
    inv_std = lax.rsqrt(jnp.mean(centred * centred, axis=-1, keepdims=True) + EPSILON)
    return centred * inv_std, inv_std


def norm_back(grad, scaled, inv_std, gain):
    grad_scaled = grad * gain
    mean_first = jnp.mean(grad_scaled, axis=-1, keepdims=True)
    mean_second = jnp.mean(grad_scaled * scaled, axis=-1, keepdims=True)
    return inv_std * (grad_scaled - mean_first - scaled * mean_second), jnp.sum(grad * scaled, axis=0, keepdims=True)


def layer_kernel(
    dp_size, mol_hbm, gain_one, wq_hbm, wk_hbm, wv_hbm, wo_hbm, gain_two, wi_hbm, wu_hbm, cot_hbm, mask_ref,
    act_out, gmol_out, sums_out, gains_out,
    x, cot, wqkv, wo, wi, wu, n1, turned, qkv, mixed, mixed_t, pin, pout, n2, gres, act, gip, lse, hid,
    gains_sum, gains_in, grads, far, line, near, beyond,
    in_sem, mp_send, mp_recv, gain_send, gain_recv, ring_send, ring_recv, ring_own,
):
    mp = lax.axis_index("mp")
    dp = lax.axis_index("dp")
    rows, width = n1.shape
    half = rows // 2
    shard = half // 2
    heads_width = wo.shape[0]
    pairs = heads_width // 128
    joined = 3 * 128
    ring = Ring(grads, far, line, near, beyond, sums_out, ring_send, ring_recv, ring_own, dp_size)
    stages = ring.stages()
    own = pl.ds(al(mp * half, half), half)
    other = pl.ds(al((1 - mp) * half, half), half)
    gbr = n2
    slot = iter(SCHEDULE)

    def advance():
        for stage, unit in next(slot, ()):
            stages[stage](unit)

    def own_of(s):
        return pl.ds(al(mp * half + s * shard, shard), shard)

    def other_of(s):
        return pl.ds(al((1 - mp) * half + s * shard, shard), shard)

    def take(ref, s, columns):
        return jnp.concatenate([ref[pl.ds(s * shard, shard), columns], ref[pl.ds(half + s * shard, shard), columns]])

    def put(ref, s, columns, values):
        ref[pl.ds(s * shard, shard), columns] = values[:shard]
        ref[pl.ds(half + s * shard, shard), columns] = values[shard:]

    def to_peer(src, dst, k):
        return pltpu.make_async_remote_copy(
            src_ref=src, dst_ref=dst, send_sem=mp_send.at[k], recv_sem=mp_recv.at[k],
            device_id=(dp, 1 - mp), device_id_type=MESH)

    def rows_copy(ref, s, k):
        return to_peer(ref.at[own_of(s)], ref.at[own_of(s)], k)

    def part_copy(kind, s):
        return to_peer(pout.at[kind % 2, s], pin.at[kind % 3, s], 8 + 2 * kind + s)

    def whole_part(kind):
        return to_peer(pout.at[kind % 2], pin.at[kind % 3], 8 + 2 * kind)

    loads = [
        pltpu.make_async_copy(mol_hbm.at[0], x.at[0], in_sem.at[0]),
        pltpu.make_async_copy(mol_hbm.at[1], x.at[1], in_sem.at[1]),
    ]
    for kind, source in enumerate((wq_hbm, wk_hbm, wv_hbm)):
        for pair in range(pairs):
            loads.append(pltpu.make_async_copy(
                source.at[:, pl.ds(pair * 128, 128)], wqkv.at[:, pl.ds(pair * joined + kind * 128, 128)],
                in_sem.at[len(loads)]))
    weights = loads[2:]
    others = []
    for source, target in ((cot_hbm, cot), (wo_hbm, wo), (wi_hbm, wi), (wu_hbm, wu)):
        others.append(pltpu.make_async_copy(source, target, in_sem.at[len(loads) + len(others)]))
    for load in loads + others:
        load.start()

    barrier = pltpu.get_barrier_semaphore()
    flips = [1, 2, 4, 8, 12] + [16 << k for k in range(ring.extra)]
    for flip in flips:
        pl.semaphore_signal(barrier, inc=1, device_id=(dp ^ flip, mp), device_id_type=MESH)
    pl.semaphore_signal(barrier, inc=1, device_id=(dp, 1 - mp), device_id_type=MESH)

    for s in range(2):
        loads[s].wait()
        scaled, _ = normalize(x[s].astype(f32))
        n1[own_of(s), :] = (scaled * gain_one[...]).astype(bf16)
        if s == 0:
            pl.semaphore_wait(barrier, len(flips) + 1)
        rows_copy(n1, s, s).start()

    others[0].wait()
    lanes = lax.broadcasted_iota(jnp.int32, (128, 128), 1)
    subs = lax.broadcasted_iota(jnp.int32, (128, 128), 0)
    for s in range(2):
        for piece in range(shard // 128):
            row = mask_ref[pl.ds(s, 1), pl.ds(piece * 128, 128)].astype(f32)
            column = jnp.sum(jnp.where(lanes == subs, row, 0.0), axis=1, keepdims=True)
            weight = 0.25 + 0.75 * column
            values = cot[s, pl.ds(piece * 128, 128), :].astype(f32) * weight
            gres[pl.ds(al(mp * half + s * shard + piece * 128, 128), 128), :] = values.astype(bf16)
        rows_copy(gres, s, 2 + s).start()

    lane = lax.broadcasted_iota(jnp.int32, (1, 128), 1)
    sides = (lane < HEAD_DIM, lane >= HEAD_DIM)
    scale = HEAD_DIM ** -0.5

    def columns(pair, kind):
        return pl.ds(pair * joined + kind * 128, 128)

    for load in weights:
        load.wait()
    qkv[own, :] = dot(n1[own, :], wqkv[...]).astype(bf16)
    for s in range(2):
        rows_copy(n1, s, s).wait_recv()
    qkv[other, :] = dot(n1[other, :], wqkv[...]).astype(bf16)
    others[1].wait()
    for s in range(2):
        logs = jnp.zeros((half, 128), f32)
        for pair in range(pairs):
            query = take(qkv, s, columns(pair, 0)) * jnp.asarray(scale, bf16)
            key = take(qkv, s, columns(pair, 1))
            value = take(qkv, s, columns(pair, 2))
            outs = []
            for side in range(2):
                scores = dot_nt(jnp.where(sides[side], query, 0), key)
                row_max = jnp.max(scores, axis=-1, keepdims=True)
                expon = jnp.exp(scores - row_max)
                total = jnp.sum(expon, axis=-1, keepdims=True)
                logs = jnp.where(lane == 2 * pair + side, row_max + jnp.log(total), logs)
                outs.append(dot(expon.astype(bf16), value) * (1.0 / total))
            put(mixed, s, pl.ds(pair * 128, 128), jnp.where(sides[0], outs[0], outs[1]).astype(bf16))
        lse[s] = logs
        pout[0, s] = dot(mixed[other_of(s), :], wo[...]).astype(bf16)
        part_copy(0, s).start()
    own_part = dot(mixed[own, :], wo[...])
    for s in range(2):
        hid[s] = x[s].astype(f32) + own_part[s * shard:(s + 1) * shard]

    for s in range(2):
        part_copy(0, s).wait_recv()
        hidden = hid[s] + pin[0, s].astype(f32)
        hid[s] = hidden
        scaled, _ = normalize(hidden)
        n2[own_of(s), :] = (scaled * gain_two[...]).astype(bf16)
        rows_copy(n2, s, 4 + s).start()
    mixed_t[...] = mixed[...].T
    turned[:, own] = n2[own, :].T
    for s in range(2):
        rows_copy(gres, s, 2 + s).wait_recv()
    others[2].wait()
    others[3].wait()
    for s in range(2):
        rows_copy(n2, s, 4 + s).wait_recv()
    turned[:, other] = n2[other, :].T

    for b in range(wi.shape[1] // BLOCK):
        block = pl.ds(b * BLOCK, BLOCK)
        inner = dot(n2[...], wi[:, block])
        shape = 1.0 + lax.erf(inner * (0.5 ** 0.5))
        active = (0.5 * inner * shape).astype(bf16)
        act[:, block] = active
        slope = 0.5 * shape + inner * (jnp.exp(-0.5 * inner * inner) * (2.0 * 3.141592653589793) ** -0.5)
        part = dot(active.T, gres[...]).astype(bf16)
        for g in range(width // 128):
            grads[b, pl.ds(g * BLOCK, BLOCK), :] = part[:, g * 128:(g + 1) * 128]
        advance()
        back = dot_nt(gres[...], wu[block, :])
        pre = (back * slope).astype(bf16)
        gip[:, block] = pre
        part = dot(turned[...], pre).astype(bf16)
        for g in range(BLOCK // 128):
            grads[b, pl.ds(width // 128 * BLOCK + g * width, width), :] = part[:, g * 128:(g + 1) * 128]
        advance()

    def send_part(kind, values):
        if kind >= 2:
            for s in range(2 if kind == 2 else 0):
                part_copy(0, s).wait_send()
            if kind == 3:
                whole_part(1).wait_send()
        for s in range(2):
            pout[kind % 2, s] = values[s * shard:(s + 1) * shard].astype(bf16)
        whole_part(kind).start()

    send_part(1, dot_nt(gip[other, :], wi[...]))
    advance()
    grad = dot_nt(gip[own, :], wi[...])
    turned[...] = n1[...].T
    advance()
    whole_part(1).wait_recv()
    gain_two_sum = jnp.zeros((1, width), f32)
    for s in range(2):
        scaled, inv_std = normalize(hid[s])
        grad_values, gain_part = norm_back(
            grad[s * shard:(s + 1) * shard] + pin[1, s].astype(f32), scaled, inv_std, gain_two[...])
        gain_two_sum += gain_part
        grad_hidden = gres[own_of(s), :].astype(f32) + grad_values
        gbr_rows = grad_hidden.astype(bf16)
        if s == 0:
            for k in range(2):
                rows_copy(n2, k, 4 + k).wait_send()
        gmol_out[s] = grad_hidden
        gbr[own_of(s), :] = gbr_rows
        rows_copy(gbr, s, 6 + s).start()
    advance()
    send_part(2, dot(act[other, :], wu[...]))
    advance()
    for s in range(2):
        rows_copy(gbr, s, 6 + s).wait_recv()
    mixed[...] = dot_nt(gbr[...], wo[...]).astype(bf16)
    advance()
    part = dot(mixed_t[...], gbr[...]).astype(bf16)
    for g in range(width // 128):
        grads[FF_UNITS + g // 2, pl.ds(3 * width + g % 2 * heads_width, heads_width), :] = part[:, g * 128:(g + 1) * 128]
    advance()

    for pair in range(pairs):
        for s in range(2):
            query = take(qkv, s, columns(pair, 0)) * jnp.asarray(scale, bf16)
            key = take(qkv, s, columns(pair, 1))
            value = take(qkv, s, columns(pair, 2))
            grad_mixed = take(mixed, s, pl.ds(pair * 128, 128))
            logs = lse[s]
            found = []
            for side in range(2):
                log_total = jnp.sum(jnp.where(lane == 2 * pair + side, logs, 0.0), axis=-1, keepdims=True)
                probs = jnp.exp(dot_nt(jnp.where(sides[side], query, 0), key) - log_total)
                grad_probs = dot_nt(jnp.where(sides[side], grad_mixed, 0), value)
                row_inner = jnp.sum(probs * grad_probs, axis=-1, keepdims=True)
                grad_scores = (probs * (grad_probs - row_inner)).astype(bf16)
                grad_value = dot_tn(probs.astype(bf16), grad_mixed)
                grad_query = dot(grad_scores, key) * scale
                grad_key = dot_tn(grad_scores, query)
                found.append((grad_query, grad_key, grad_value))
            for kind in range(3):
                put(gip, s, columns(pair, kind), jnp.where(sides[0], found[0][kind], found[1][kind]).astype(bf16))
            advance()
        part = dot(turned[...], gip[:, pl.ds(pair * joined, joined)]).astype(bf16)
        for kind in range(3):
            grads[FF_UNITS + pair, pl.ds(kind * width, width), :] = part[:, kind * 128:(kind + 1) * 128]
        advance()

    all_joined = pl.ds(0, pairs * joined)
    send_part(3, dot_nt(gip[other, all_joined], wqkv[...]))
    advance()
    grad = dot_nt(gip[own, all_joined], wqkv[...])
    advance()
    result = dot(act[own, :], wu[...])
    whole_part(2).wait_recv()
    for s in range(2):
        act_out[s] = (hid[s] + result[s * shard:(s + 1) * shard] + pin[2, s].astype(f32)).astype(bf16)
    advance()
    whole_part(3).wait_recv()
    gain_one_sum = jnp.zeros((1, width), f32)
    for s in range(2):
        scaled, inv_std = normalize(x[s].astype(f32))
        grad_values, gain_part = norm_back(
            grad[s * shard:(s + 1) * shard] + pin[0, s].astype(f32), scaled, inv_std, gain_one[...])
        gain_one_sum += gain_part
        gmol_out[s] = gmol_out[s] + grad_values
    gains_sum[0] = jnp.zeros(gains_sum.shape[1:], f32)
    for g in range(width // 128):
        gains_sum[0, pl.ds(g, 1), :] = gain_one_sum[:, g * 128:(g + 1) * 128]
        gains_sum[0, pl.ds(8 + g, 1), :] = gain_two_sum[:, g * 128:(g + 1) * 128]

    targets = [(dp, 1 - mp)] + [(dp ^ (1 << k), mp) for k in range(4 + ring.extra)]

    def gain_copy(k):
        return pltpu.make_async_remote_copy(
            src_ref=gains_sum.at[k], dst_ref=gains_in.at[k], send_sem=gain_send.at[k], recv_sem=gain_recv.at[k],
            device_id=targets[k], device_id_type=MESH)

    def gain_step(k):
        if k:
            gain_copy(k - 1).wait_recv()
            total = gains_sum[k - 1] + gains_in[k - 1]
            if k == len(targets):
                gains_out[...] = total
            else:
                gains_sum[k] = total
        if k < len(targets):
            gain_copy(k).start()

    tail = [step for part in slot for step in part]
    steps = len(targets) + 1
    for i, (stage, unit) in enumerate(tail):
        if i % 3 == 0 and i // 3 < steps:
            gain_step(i // 3)
        stages[stage](unit)
    for k in range((len(tail) + 2) // 3, steps):
        gain_step(k)

    for s in range(2):
        rows_copy(n1, s, s).wait_send()
        rows_copy(gres, s, 2 + s).wait_send()
        rows_copy(gbr, s, 6 + s).wait_send()
    for kind in (2, 3):
        whole_part(kind).wait_send()
    for k in range(len(targets)):
        gain_copy(k).wait_send()
    for u in range(UNITS):
        ring.sent(u)


def finish_kernel(
    act_in, gmol_in, packed, act_out, gmol_out, gq, gk, gv, go, gi, gu,
    query, key, value, output, inner, outer, out_sem,
):
    width, heads_width = query.shape
    outs = []

    def send(src, dst):
        copy = pltpu.make_async_copy(src, dst, out_sem.at[len(outs)])
        copy.start()
        outs.append(copy)
    send(act_in, act_out)
    send(gmol_in, gmol_out)
    at = width // 128 * BLOCK
    for b in range(FF_UNITS):
        for g in range(width // 128):
            outer[pl.ds(b * BLOCK, BLOCK), pl.ds(g * 128, 128)] = packed[b, pl.ds(g * BLOCK, BLOCK), :].astype(f32)
        send(outer.at[pl.ds(b * BLOCK, BLOCK)], gu.at[pl.ds(b * BLOCK, BLOCK)])
        for g in range(BLOCK // 128):
            inner[:, pl.ds(b * BLOCK + g * 128, 128)] = packed[b, pl.ds(at + g * width, width), :].astype(f32)
        send(inner.at[:, pl.ds(b * BLOCK, BLOCK)], gi.at[:, pl.ds(b * BLOCK, BLOCK)])
    for kind, block in enumerate((query, key, value)):
        for pair in range(heads_width // 128):
            block[:, pl.ds(pair * 128, 128)] = packed[FF_UNITS + pair, pl.ds(kind * width, width), :].astype(f32)
        send(block, (gq, gk, gv)[kind])
    for g in range(width // 128):
        output[:, pl.ds(g * 128, 128)] = packed[
            FF_UNITS + g // 2, pl.ds(3 * width + g % 2 * heads_width, heads_width), :].astype(f32)
    send(output, go)
    for copy in outs:
        copy.wait()


ANY = pl.BlockSpec(memory_space=pl.ANY)
WHOLE = pl.BlockSpec(memory_space=pltpu.VMEM)


def per_device(
    dp_size, molecules, gain_attn, w_query, w_key, w_value, w_output, gain_ffn, w_inner, w_outer, cotangent, span_mask
):
    count, shard, width = molecules.shape
    heads_width = w_query.shape[1]
    units_inner = w_inner.shape[1]
    rows = 2 * count * shard
    extra = (dp_size // 16).bit_length() - 1
    levels = 5 + extra
    act, gmol, sums, gains = pl.pallas_call(
        functools.partial(layer_kernel, dp_size),
        out_shape=(
            pltpu.VMEM(molecules.shape, bf16),
            pltpu.VMEM(molecules.shape, f32),
            pltpu.VMEM((UNITS, ROWS, 128), bf16),
            jax.ShapeDtypeStruct((16, 128), f32),
        ),
        in_specs=[ANY, WHOLE, ANY, ANY, ANY, ANY, WHOLE, ANY, ANY, ANY, WHOLE],
        out_specs=(WHOLE, WHOLE, WHOLE, WHOLE),
        scratch_shapes=[
            pltpu.VMEM(molecules.shape, bf16),
            pltpu.VMEM(molecules.shape, bf16),
            pltpu.VMEM((width, 3 * heads_width), bf16),
            pltpu.VMEM(w_output.shape, bf16),
            pltpu.VMEM(w_inner.shape, bf16),
            pltpu.VMEM(w_outer.shape, bf16),
            pltpu.VMEM((rows, width), bf16),
            pltpu.VMEM((width, rows), bf16),
            pltpu.VMEM((rows, 3 * heads_width), bf16),
            pltpu.VMEM((rows, heads_width), bf16),
            pltpu.VMEM((heads_width, rows), bf16),
            pltpu.VMEM((3,) + molecules.shape, bf16),
            pltpu.VMEM((2,) + molecules.shape, bf16),
            pltpu.VMEM((rows, width), bf16),
            pltpu.VMEM((rows, width), bf16),
            pltpu.VMEM((rows, units_inner), bf16),
            pltpu.VMEM((rows, units_inner), bf16),
            pltpu.VMEM((count, rows // 2, 128), f32),
            pltpu.VMEM(molecules.shape, f32),
            pltpu.VMEM((levels, 16, 128), f32),
            pltpu.VMEM((levels, 16, 128), f32),
            pltpu.VMEM((UNITS, ROWS, 128), bf16),
            pltpu.VMEM((UNITS, 2, QUAD, 128), bf16),
            pltpu.VMEM((UNITS, 2, QUAD, 128), bf16),
            pltpu.VMEM((UNITS, 2, PART, 128), bf16),
            pltpu.VMEM((UNITS if extra else 1, 2, max(extra, 1), PART, 128), bf16),
            pltpu.SemaphoreType.DMA((15,)),
            pltpu.SemaphoreType.DMA((16,)),
            pltpu.SemaphoreType.DMA((16,)),
            pltpu.SemaphoreType.DMA((levels,)),
            pltpu.SemaphoreType.DMA((levels,)),
            pltpu.SemaphoreType.DMA((UNITS, 6 + 2 * extra)),
            pltpu.SemaphoreType.DMA((UNITS, 6 + 2 * extra)),
            pltpu.SemaphoreType.DMA((UNITS,)),
        ],
        compiler_params=pltpu.CompilerParams(
            collective_id=0, has_side_effects=True, vmem_limit_bytes=VMEM_LIMIT),
        name="layer",
    )(
        molecules, gain_attn.reshape(1, -1), w_query, w_key, w_value, w_output, gain_ffn.reshape(1, -1),
        w_inner, w_outer, cotangent, span_mask,
    )
    shapes = [jax.ShapeDtypeStruct(w.shape, f32) for w in (w_query, w_key, w_value, w_output, w_inner, w_outer)]
    outs = pl.pallas_call(
        finish_kernel,
        out_shape=(
            jax.ShapeDtypeStruct(molecules.shape, bf16), jax.ShapeDtypeStruct(molecules.shape, f32), *shapes),
        in_specs=[WHOLE] * 3,
        out_specs=(ANY,) * 8,
        scratch_shapes=[pltpu.VMEM(shape.shape, f32) for shape in shapes]
        + [pltpu.SemaphoreType.DMA((2 + 2 * FF_UNITS + 4,))],
        compiler_params=pltpu.CompilerParams(vmem_limit_bytes=40 * 2 ** 20),
        name="finish",
    )(act, gmol, sums)
    return (*outs, gains[0:6].reshape(width), gains[8:14].reshape(width))


def solution(mesh):
    in_specs = (
        P("dp", "mp", None),
        P(),
        P(None, "mp"),
        P(None, "mp"),
        P(None, "mp"),
        P("mp", None),
        P(),
        P(None, "mp"),
        P("mp", None),
        P("dp", "mp", None),
        P("dp", "mp"),
    )
    out_specs = (
        P("dp", "mp", None),
        P("dp", "mp", None),
        P(None, "mp"),
        P(None, "mp"),
        P(None, "mp"),
        P("mp", None),
        P(None, "mp"),
        P("mp", None),
        P(),
        P(),
    )
    return jax.shard_map(
        functools.partial(per_device, mesh.shape["dp"]),
        mesh=mesh, in_specs=in_specs, out_specs=out_specs, check_vma=False,
    )
```

```python
import functools

import jax
import jax.numpy as jnp
from jax import lax
from jax.experimental import pallas as pl
from jax.experimental.pallas import tpu as pltpu
from jax.sharding import PartitionSpec as P

HEAD_DIM = 64
EPSILON = 1e-05
MESH = pl.DeviceIdType.MESH
bf16 = jnp.bfloat16
f32 = jnp.float32

ROWS = 1536
HALF = ROWS // 2
QUAD = HALF // 2
SIDE = QUAD // 2
PART = SIDE // 2
FF_UNITS = 12
UNITS = 18
BLOCK = 256
GAIN_SPACING = 10


VMEM_LIMIT = 54 * 2 ** 20

SCHEDULE = (
    ((0, 0),),
    ((0, 1),),
    ((0, 2),),
    ((1, 0), (0, 3),),
    ((1, 1), (0, 4),),
    ((0, 5),),
    ((2, 0), (1, 2), (0, 6),),
    ((2, 1), (1, 3), (0, 7),),
    ((1, 4), (0, 8),),
    ((3, 0), (2, 2), (0, 9), (1, 5),),
    ((2, 3), (3, 1), (1, 6), (0, 10),),
    ((2, 4), (0, 11),),
    ((4, 0), (2, 5), (3, 2), (1, 7),),
    ((3, 3), (4, 1), (3, 4), (2, 6), (1, 9), (1, 8),),
    ((3, 5), (4, 2), (2, 7), (1, 10), (1, 11), (5, 0), (2, 9),),
    ((5, 1), (4, 3), (3, 6), (2, 8),),
    ((5, 2), (6, 0), (4, 4), (3, 7), (2, 10),),
    ((6, 1), (5, 3), (4, 5), (0, 12),),
    ((7, 0), (6, 2), (6, 3), (3, 9), (4, 6), (5, 4), (5, 5), (2, 11), (3, 8),),
    ((7, 1), (4, 7), (5, 6), (3, 10), (6, 4), (7, 2), (1, 12),),
    ((8, 0), (0, 13), (6, 5), (0, 14),),
    ((7, 4), (5, 7), (7, 3), (4, 8), (3, 11), (4, 9), (6, 6), (8, 1),),
    ((8, 2), (4, 10), (1, 13), (9, 0), (2, 12), (7, 5),),
    ((8, 4), (5, 8), (6, 7), (5, 9), (0, 15),),
    ((9, 1), (8, 3), (10, 0), (2, 13), (7, 6), (4, 11), (5, 10), (1, 14), (3, 12),),
    ((9, 2), (8, 5), (6, 9), (7, 7), (6, 8), (9, 4),),
    ((0, 16), (2, 14), (0, 17), (3, 13),),
    ((9, 3), (10, 1), (8, 6), (5, 11), (6, 10), (1, 15), (7, 9),),
    ((10, 2), (4, 12),),
    ((7, 8), (10, 4), (9, 5), (8, 7),),
    ((4, 13), (3, 14), (1, 16), (9, 6), (2, 15), (7, 10), (8, 9), (1, 17), (8, 8), (9, 7), (10, 3), (6, 11),
     (5, 12), (4, 14), (10, 5), (5, 13), (9, 9), (10, 6), (9, 8), (2, 16), (3, 15), (2, 17), (8, 10), (7, 11),
     (3, 16), (10, 7), (4, 15), (6, 12), (5, 14), (6, 13), (9, 10), (10, 9), (4, 16), (10, 8), (5, 15), (6, 14),
     (3, 17), (4, 17), (10, 10), (5, 16), (6, 15), (5, 17), (6, 16), (6, 17), (8, 11), (9, 11), (7, 12), (7, 13),
     (8, 12), (9, 12), (8, 13), (7, 14), (9, 13), (10, 11), (10, 12), (7, 15), (8, 14), (9, 14), (7, 16), (8, 15),
     (7, 17), (8, 16), (10, 13), (9, 15), (10, 14), (9, 16), (10, 15), (8, 17), (9, 17), (10, 16), (10, 17),),
)


def al(v, m):
    return pl.multiple_of(v, m)


class Ring:
    def __init__(self, grads, far, line, near, beyond, out, send_sem, recv_sem, own_sem, dp_size):
        self.grads, self.far, self.line, self.near, self.beyond, self.out = grads, far, line, near, beyond, out
        self.send_sem, self.recv_sem, self.own_sem = send_sem, recv_sem, own_sem
        self.extra = (dp_size // 16).bit_length() - 1
        self.dp = lax.axis_index("dp")
        self.mp = lax.axis_index("mp")
        place = lax.rem(lax.div(self.dp, 4), 4)
        low = jnp.where(place < 2, 1, 0)
        self.is_end = (place == 0) | (place == 3)
        self.is_mid = (place == 1) | (place == 2)
        self.inward = self.dp + 4 * (2 * low - 1)
        self.outward = self.dp - 4 * (2 * low - 1)
        self.far_side = low * SIDE
        self.own_side = (1 - low) * SIDE
        bits = (lax.rem(self.dp, 2), lax.rem(lax.div(self.dp, 2), 2))
        self.first_bit = bits
        self.last_bit = (bits[1], bits[0])
        self.first_peer = [self.dp + (1 - 2 * bits[h]) * (1 << h) for h in range(2)]
        self.last_peer = [self.first_peer[1], self.first_peer[0]]

    def kept(self, h, offset, count):
        return pl.ds(al(h * HALF + self.first_bit[h] * QUAD + offset, 16), count)

    def side(self, offset, count=SIDE):
        return pl.ds(al(offset, 16), count)

    def copy(self, src, dst, u, sent, received, dp):
        return pltpu.make_async_remote_copy(
            src_ref=src, dst_ref=dst, send_sem=self.send_sem.at[sent], recv_sem=self.recv_sem.at[u, received],
            device_id=(dp, self.mp), device_id_type=MESH)

    def received(self, block, u, k):
        self.copy(block, block, u, k, k, self.first_peer[0]).wait_recv()

    def was_sent(self, block, k):
        self.copy(block, block, 0, k, 0, self.first_peer[0]).wait_send()

    def add(self, u, rows, other):
        self.grads[u, rows] = (self.grads[u, rows].astype(f32) + other.astype(f32)).astype(bf16)

    def pass_sum(self, u, offset, sent, received, dp):
        for h in range(2):
            self.copy(self.grads.at[u, self.kept(h, offset, SIDE)], self.line.at[u, h, self.side(offset)],
                      u, sent, received, dp).start()

    def take_sum(self, u, offset, received):
        self.received(self.line.at[u, :, self.side(offset)], u, received)
        for h in range(2):
            self.add(u, self.kept(h, offset, SIDE), self.line[u, h, self.side(offset)])

    def pass_whole(self, u, offset, sent, received, dp):
        for h in range(2):
            block = self.far.at[u, h, self.side(offset)]
            self.copy(block, block, u, sent, received, dp).start()

    def take_whole(self, u, offset, received):
        self.received(self.far.at[u, :, self.side(offset)], u, received)

    def finish(self, u):
        for h in range(2):
            rows = self.kept(h, 0, QUAD)
            self.copy(self.far.at[u, h], self.out.at[u, rows], u, 5, 5, self.first_peer[h]).start()
            pltpu.make_async_copy(self.far.at[u, h], self.out.at[u, rows], self.own_sem.at[0]).start()

    def stage0(self, u):
        for h in range(2):
            rows = pl.ds(al(h * HALF + (1 - self.first_bit[h]) * QUAD, 16), QUAD)
            self.copy(self.grads.at[u, rows], self.far.at[u, h], u, 0, 0, self.first_peer[h]).start()

    def stage1(self, u):
        self.received(self.far.at[u], u, 0)
        for h in range(2):
            self.add(u, self.kept(h, 0, QUAD), self.far[u, h])

        @pl.when(self.is_end)
        def _():
            self.pass_sum(u, self.far_side, 1, 1, self.inward)

    def stage2(self, u):
        @pl.when(self.is_mid)
        def _():
            self.take_sum(u, self.far_side, 1)
            self.pass_sum(u, self.far_side, 1, 2, self.inward)

    def stage3(self, u):
        @pl.when(self.is_mid)
        def _():
            self.take_sum(u, self.own_side, 2)
            self.pass_sum(u, self.own_side, 2, 2, self.outward)

    def stage4(self, u):
        @pl.when(self.is_end)
        def _():
            self.take_sum(u, self.own_side, 2)
            for h in range(2):
                rows = self.kept(h, self.own_side + (1 - self.last_bit[h]) * PART, PART)
                self.copy(self.grads.at[u, rows], self.near.at[u, h], u, 2, 1, self.last_peer[h]).start()

    def stage5(self, u):
        @pl.when(self.is_end)
        def _():
            self.received(self.near.at[u], u, 1)
            for h in range(2):
                offset = self.own_side + self.last_bit[h] * PART
                mine = self.kept(h, offset, PART)
                last = self.near[u, h]
                for k in range(self.extra):
                    self.add(u, mine, last)
                    copy = self.copy(self.grads.at[u, mine], self.beyond.at[u, h, k], u, 6 + 2 * k + h, 6 + 2 * k + h,
                                     self.dp ^ (16 << k))
                    copy.start()
                    copy.wait()
                    last = self.beyond[u, h, k]
                rows = self.side(offset, PART)
                self.far[u, h, rows] = (self.grads[u, mine].astype(f32) + last.astype(f32)).astype(bf16)
                block = self.far.at[u, h, rows]
                self.copy(block, block, u, 3, 3, self.last_peer[h]).start()

    def stage6(self, u):
        @pl.when(self.is_end)
        def _():
            self.received(self.near.at[u], u, 3)
            self.pass_whole(u, self.own_side, 4, 3, self.inward)

    def stage7(self, u):
        @pl.when(self.is_mid)
        def _():
            self.take_whole(u, self.own_side, 3)
            self.pass_whole(u, self.own_side, 3, 4, self.inward)

    def stage8(self, u):
        @pl.when(self.is_mid)
        def _():
            self.take_whole(u, self.far_side, 4)
            self.pass_whole(u, self.far_side, 4, 4, self.outward)
            self.finish(u)

    def stage9(self, u):
        @pl.when(self.is_end)
        def _():
            self.take_whole(u, self.far_side, 4)
            self.finish(u)

    def stage10(self, u):
        self.received(self.far.at[u], u, 5)

    def sent(self):
        self.was_sent(self.far, 0)
        self.was_sent(self.far, 5)
        pltpu.make_async_copy(self.far, self.far, self.own_sem.at[0]).wait()
        one_side = self.line.at[:, :, pl.ds(0, SIDE)]

        @pl.when(self.is_end)
        def _():
            for k, block in ((1, one_side), (2, self.near), (3, self.near), (4, one_side)):
                self.was_sent(block, k)

        @pl.when(self.is_mid)
        def _():
            for k in range(1, 5):
                self.was_sent(one_side, k)

    def stages(self):
        return (self.stage0, self.stage1, self.stage2, self.stage3, self.stage4, self.stage5, self.stage6,
                self.stage7, self.stage8, self.stage9, self.stage10)


def dot(a, b):
    return jnp.dot(a, b, preferred_element_type=f32)


def dot_nt(a, b):
    return lax.dot_general(a, b, (((1,), (1,)), ((), ())), preferred_element_type=f32)


def dot_tn(a, b):
    return lax.dot_general(a, b, (((0,), (0,)), ((), ())), preferred_element_type=f32)


def normalize(values):
    centred = values - jnp.mean(values, axis=-1, keepdims=True)
    inv_std = lax.rsqrt(jnp.mean(centred * centred, axis=-1, keepdims=True) + EPSILON)
    return centred * inv_std, inv_std


def norm_back(grad, scaled, inv_std, gain):
    grad_scaled = grad * gain
    mean_first = jnp.mean(grad_scaled, axis=-1, keepdims=True)
    mean_second = jnp.mean(grad_scaled * scaled, axis=-1, keepdims=True)
    return inv_std * (grad_scaled - mean_first - scaled * mean_second), jnp.sum(grad * scaled, axis=0, keepdims=True)


def layer_kernel(
    dp_size, mol_hbm, gain_one_hbm, wq_hbm, wk_hbm, wv_hbm, wo_hbm, gain_two_hbm, wi_hbm, wu_hbm, cot_hbm, mask_ref,
    act_out, gmol_out, sums_out, gains_out,
    gains, x, cot, wqkv, wo, wi, wu, n1, turned, qkv, mixed, mixed_t, pin, pout, n2, gres, act, gip, lse, hid,
    gains_sum, gains_in, grads, far, line, near, beyond,
    in_sem, mp_send, mp_recv, gain_send, gain_recv, ring_send, ring_recv, ring_own,
):
    mp = lax.axis_index("mp")
    dp = lax.axis_index("dp")
    rows, width = n1.shape
    half = rows // 2
    shard = half // 2
    heads_width = wo.shape[0]
    pairs = heads_width // 128
    joined = 3 * 128
    ring = Ring(grads, far, line, near, beyond, sums_out, ring_send, ring_recv, ring_own, dp_size)
    stages = ring.stages()
    own = pl.ds(al(mp * half, half), half)
    other = pl.ds(al((1 - mp) * half, half), half)
    gbr = n2
    slot = iter(SCHEDULE)

    def advance():
        for stage, unit in next(slot, ()):
            stages[stage](unit)

    def own_of(s):
        return pl.ds(al(mp * half + s * shard, shard), shard)

    def other_of(s):
        return pl.ds(al((1 - mp) * half + s * shard, shard), shard)

    def take(ref, s, columns):
        return jnp.concatenate([ref[pl.ds(s * shard, shard), columns], ref[pl.ds(half + s * shard, shard), columns]])

    def put(ref, s, columns, values):
        ref[pl.ds(s * shard, shard), columns] = values[:shard]
        ref[pl.ds(half + s * shard, shard), columns] = values[shard:]

    def to_peer(src, dst, k):
        return pltpu.make_async_remote_copy(
            src_ref=src, dst_ref=dst, send_sem=mp_send.at[k], recv_sem=mp_recv.at[k],
            device_id=(dp, 1 - mp), device_id_type=MESH)

    def rows_copy(ref, s, k):
        return to_peer(ref.at[own_of(s)], ref.at[own_of(s)], k)

    def part_copy(kind, s):
        return to_peer(pout.at[kind % 2, s], pin.at[kind % 3, s], 8 + 2 * kind + s)

    def whole_part(kind):
        return to_peer(pout.at[kind % 2], pin.at[kind % 3], 8 + 2 * kind)

    gain_one = gains.at[pl.ds(0, 1)]
    gain_two = gains.at[pl.ds(1, 1)]

    loads = [
        pltpu.make_async_copy(mol_hbm.at[0], x.at[0], in_sem.at[0]),
        pltpu.make_async_copy(mol_hbm.at[1], x.at[1], in_sem.at[1]),
    ]
    for kind, source in enumerate((wq_hbm, wk_hbm, wv_hbm)):
        for pair in range(pairs):
            loads.append(pltpu.make_async_copy(
                source.at[:, pl.ds(pair * 128, 128)], wqkv.at[:, pl.ds(pair * joined + kind * 128, 128)],
                in_sem.at[len(loads)]))
    weights = loads[2:]
    others = []
    for source, target in ((cot_hbm, cot), (wo_hbm, wo), (wi_hbm, wi), (wu_hbm, wu)):
        others.append(pltpu.make_async_copy(source, target, in_sem.at[len(loads) + len(others)]))
    gain_loads = [
        pltpu.make_async_copy(source, gains.at[k], in_sem.at[len(loads) + len(others) + k])
        for k, source in enumerate((gain_one_hbm, gain_two_hbm))
    ]
    for load in gain_loads + loads + others:
        load.start()

    barrier = pltpu.get_barrier_semaphore()
    flips = [1, 2, 4, 8, 12] + [16 << k for k in range(ring.extra)]
    for flip in flips:
        pl.semaphore_signal(barrier, inc=1, device_id=(dp ^ flip, mp), device_id_type=MESH)
    pl.semaphore_signal(barrier, inc=1, device_id=(dp, 1 - mp), device_id_type=MESH)

    for load in gain_loads:
        load.wait()
    for s in range(2):
        loads[s].wait()
        scaled, _ = normalize(x[s].astype(f32))
        n1[own_of(s), :] = (scaled * gain_one[...]).astype(bf16)
        if s == 0:
            pl.semaphore_wait(barrier, len(flips) + 1)
        rows_copy(n1, s, s).start()

    others[0].wait()
    lanes = lax.broadcasted_iota(jnp.int32, (128, 128), 1)
    subs = lax.broadcasted_iota(jnp.int32, (128, 128), 0)
    for s in range(2):
        for piece in range(shard // 128):
            row = mask_ref[pl.ds(s, 1), pl.ds(piece * 128, 128)].astype(f32)
            column = jnp.sum(jnp.where(lanes == subs, row, 0.0), axis=1, keepdims=True)
            weight = 0.25 + 0.75 * column
            values = cot[s, pl.ds(piece * 128, 128), :].astype(f32) * weight
            gres[pl.ds(al(mp * half + s * shard + piece * 128, 128), 128), :] = values.astype(bf16)
        rows_copy(gres, s, 2 + s).start()

    lane = lax.broadcasted_iota(jnp.int32, (1, 128), 1)
    sides = (lane < HEAD_DIM, lane >= HEAD_DIM)
    scale = HEAD_DIM ** -0.5

    def columns(pair, kind):
        return pl.ds(pair * joined + kind * 128, 128)

    for load in weights:
        load.wait()
    qkv[own, :] = dot(n1[own, :], wqkv[...]).astype(bf16)
    for s in range(2):
        rows_copy(n1, s, s).wait_recv()
    qkv[other, :] = dot(n1[other, :], wqkv[...]).astype(bf16)
    others[1].wait()
    for s in range(2):
        logs = jnp.zeros((half, 128), f32)
        for pair in range(pairs):
            query = take(qkv, s, columns(pair, 0)) * jnp.asarray(scale, bf16)
            key = take(qkv, s, columns(pair, 1))
            value = take(qkv, s, columns(pair, 2))
            outs = []
            for side in range(2):
                scores = dot_nt(jnp.where(sides[side], query, 0), key)
                row_max = jnp.max(scores, axis=-1, keepdims=True)
                expon = jnp.exp(scores - row_max)
                total = jnp.sum(expon, axis=-1, keepdims=True)
                logs = jnp.where(lane == 2 * pair + side, row_max + jnp.log(total), logs)
                outs.append(dot(expon.astype(bf16), value) * (1.0 / total))
            put(mixed, s, pl.ds(pair * 128, 128), jnp.where(sides[0], outs[0], outs[1]).astype(bf16))
        lse[s] = logs
        pout[0, s] = dot(mixed[other_of(s), :], wo[...]).astype(bf16)
        part_copy(0, s).start()
    own_part = dot(mixed[own, :], wo[...])
    for s in range(2):
        hid[s] = x[s].astype(f32) + own_part[s * shard:(s + 1) * shard]

    for s in range(2):
        part_copy(0, s).wait_recv()
        hidden = hid[s] + pin[0, s].astype(f32)
        hid[s] = hidden
        scaled, _ = normalize(hidden)
        n2[own_of(s), :] = (scaled * gain_two[...]).astype(bf16)
        rows_copy(n2, s, 4 + s).start()
    mixed_t[...] = mixed[...].T
    turned[:, own] = n2[own, :].T
    for s in range(2):
        rows_copy(gres, s, 2 + s).wait_recv()
    others[2].wait()
    others[3].wait()
    for s in range(2):
        rows_copy(n2, s, 4 + s).wait_recv()
    turned[:, other] = n2[other, :].T

    for b in range(wi.shape[1] // BLOCK):
        block = pl.ds(b * BLOCK, BLOCK)
        inner = dot(n2[...], wi[:, block])
        shape = 1.0 + lax.erf(inner * (0.5 ** 0.5))
        active = (0.5 * inner * shape).astype(bf16)
        act[:, block] = active
        slope = 0.5 * shape + inner * (jnp.exp(-0.5 * inner * inner) * (2.0 * 3.141592653589793) ** -0.5)
        part = dot(active.T, gres[...]).astype(bf16)
        for g in range(width // 128):
            grads[2 * b, pl.ds(g * BLOCK, BLOCK), :] = part[:, g * 128:(g + 1) * 128]
        advance()
        back = dot_nt(gres[...], wu[block, :])
        pre = (back * slope).astype(bf16)
        gip[:, block] = pre
        part = dot(turned[...], pre).astype(bf16)
        for g in range(BLOCK // 128):
            grads[2 * b + 1, pl.ds(g * width, width), :] = part[:, g * 128:(g + 1) * 128]
        advance()

    def send_part(kind, values):
        if kind >= 2:
            for s in range(2 if kind == 2 else 0):
                part_copy(0, s).wait_send()
            if kind == 3:
                whole_part(1).wait_send()
        for s in range(2):
            pout[kind % 2, s] = values[s * shard:(s + 1) * shard].astype(bf16)
        whole_part(kind).start()

    send_part(1, dot_nt(gip[other, :], wi[...]))
    advance()
    grad = dot_nt(gip[own, :], wi[...])
    turned[...] = n1[...].T
    advance()
    whole_part(1).wait_recv()
    gain_two_sum = jnp.zeros((1, width), f32)
    for s in range(2):
        scaled, inv_std = normalize(hid[s])
        grad_values, gain_part = norm_back(
            grad[s * shard:(s + 1) * shard] + pin[1, s].astype(f32), scaled, inv_std, gain_two[...])
        gain_two_sum += gain_part
        grad_hidden = gres[own_of(s), :].astype(f32) + grad_values
        gbr_rows = grad_hidden.astype(bf16)
        if s == 0:
            for k in range(2):
                rows_copy(n2, k, 4 + k).wait_send()
        gmol_out[s] = grad_hidden
        gbr[own_of(s), :] = gbr_rows
        rows_copy(gbr, s, 6 + s).start()
    advance()
    send_part(2, dot(act[other, :], wu[...]))
    advance()
    for s in range(2):
        rows_copy(gbr, s, 6 + s).wait_recv()
    mixed[...] = dot_nt(gbr[...], wo[...]).astype(bf16)
    advance()
    part = dot(mixed_t[...], gbr[...]).astype(bf16)
    for g in range(width // 128):
        at = g * heads_width
        grads[FF_UNITS + at // ROWS, pl.ds(at % ROWS, heads_width), :] = part[:, g * 128:(g + 1) * 128]
    advance()

    for pair in range(pairs):
        for s in range(2):
            query = take(qkv, s, columns(pair, 0)) * jnp.asarray(scale, bf16)
            key = take(qkv, s, columns(pair, 1))
            value = take(qkv, s, columns(pair, 2))
            grad_mixed = take(mixed, s, pl.ds(pair * 128, 128))
            logs = lse[s]
            found = []
            for side in range(2):
                log_total = jnp.sum(jnp.where(lane == 2 * pair + side, logs, 0.0), axis=-1, keepdims=True)
                probs = jnp.exp(dot_nt(jnp.where(sides[side], query, 0), key) - log_total)
                grad_probs = dot_nt(jnp.where(sides[side], grad_mixed, 0), value)
                row_inner = jnp.sum(probs * grad_probs, axis=-1, keepdims=True)
                grad_scores = (probs * (grad_probs - row_inner)).astype(bf16)
                grad_value = dot_tn(probs.astype(bf16), grad_mixed)
                grad_query = dot(grad_scores, key) * scale
                grad_key = dot_tn(grad_scores, query)
                found.append((grad_query, grad_key, grad_value))
            for kind in range(3):
                put(gip, s, columns(pair, kind), jnp.where(sides[0], found[0][kind], found[1][kind]).astype(bf16))
            advance()
        part = dot(turned[...], gip[:, pl.ds(pair * joined, joined)]).astype(bf16)
        for kind in range(3):
            at = width // 128 * heads_width + (pair * 3 + kind) * width
            grads[FF_UNITS + at // ROWS, pl.ds(at % ROWS, width), :] = part[:, kind * 128:(kind + 1) * 128]
        advance()

    all_joined = pl.ds(0, pairs * joined)
    send_part(3, dot_nt(gip[other, all_joined], wqkv[...]))
    advance()
    grad = dot_nt(gip[own, all_joined], wqkv[...])
    advance()
    result = dot(act[own, :], wu[...])
    whole_part(2).wait_recv()
    for s in range(2):
        act_out[s] = (hid[s] + result[s * shard:(s + 1) * shard] + pin[2, s].astype(f32)).astype(bf16)
    advance()
    whole_part(3).wait_recv()
    gain_one_sum = jnp.zeros((1, width), f32)
    for s in range(2):
        scaled, inv_std = normalize(x[s].astype(f32))
        grad_values, gain_part = norm_back(
            grad[s * shard:(s + 1) * shard] + pin[0, s].astype(f32), scaled, inv_std, gain_one[...])
        gain_one_sum += gain_part
        gmol_out[s] = gmol_out[s] + grad_values
    gains_sum[0] = jnp.zeros(gains_sum.shape[1:], f32)
    gains_sum[0, pl.ds(0, 1), :] = gain_one_sum
    gains_sum[0, pl.ds(1, 1), :] = gain_two_sum

    targets = [(dp, 1 - mp)] + [(dp ^ (1 << k), mp) for k in range(4 + ring.extra)]

    def gain_copy(k):
        return pltpu.make_async_remote_copy(
            src_ref=gains_sum.at[k], dst_ref=gains_in.at[k], send_sem=gain_send.at[k], recv_sem=gain_recv.at[k],
            device_id=targets[k], device_id_type=MESH)

    def gain_step(k):
        if k:
            gain_copy(k - 1).wait_recv()
            total = gains_sum[k - 1] + gains_in[k - 1]
            if k == len(targets):
                gains_out[...] = total
            else:
                gains_sum[k] = total
        if k < len(targets):
            gain_copy(k).start()

    tail = [step for part in slot for step in part]
    steps = len(targets) + 1
    for i, (stage, unit) in enumerate(tail):
        if i % GAIN_SPACING == 0 and i // GAIN_SPACING < steps:
            gain_step(i // GAIN_SPACING)
        stages[stage](unit)
    for k in range(-(-len(tail) // GAIN_SPACING), steps):
        gain_step(k)

    for s in range(2):
        rows_copy(n1, s, s).wait_send()
        rows_copy(gres, s, 2 + s).wait_send()
        rows_copy(gbr, s, 6 + s).wait_send()
    for kind in (2, 3):
        whole_part(kind).wait_send()
    for k in range(len(targets)):
        gain_copy(k).wait_send()
    ring.sent()


def finish_kernel(
    act_in, gmol_in, packed, gains_in, act_out, gmol_out, gq, gk, gv, go, gi, gu, gain_one_out, gain_two_out,
    query, key, value, output, inner, outer, out_sem,
):
    width, heads_width = query.shape
    outs = []

    def send(src, dst):
        copy = pltpu.make_async_copy(src, dst, out_sem.at[len(outs)])
        copy.start()
        outs.append(copy)
    send(act_in, act_out)
    send(gmol_in, gmol_out)
    send(gains_in.at[0], gain_one_out)
    send(gains_in.at[1], gain_two_out)
    for b in range(FF_UNITS // 2):
        for g in range(width // 128):
            outer[pl.ds(b * BLOCK, BLOCK), pl.ds(g * 128, 128)] = packed[2 * b, pl.ds(g * BLOCK, BLOCK), :].astype(f32)
        send(outer.at[pl.ds(b * BLOCK, BLOCK)], gu.at[pl.ds(b * BLOCK, BLOCK)])
        for g in range(BLOCK // 128):
            inner[:, pl.ds(b * BLOCK + g * 128, 128)] = packed[2 * b + 1, pl.ds(g * width, width), :].astype(f32)
        send(inner.at[:, pl.ds(b * BLOCK, BLOCK)], gi.at[:, pl.ds(b * BLOCK, BLOCK)])
    at = FF_UNITS * ROWS

    def unpack(block, g, at):
        count = block.shape[0]
        block[:, pl.ds(g * 128, 128)] = packed[at // ROWS, pl.ds(at % ROWS, count), :].astype(f32)
        return at + count
    for g in range(width // 128):
        at = unpack(output, g, at)
    send(output, go)
    for pair in range(heads_width // 128):
        for block in (query, key, value):
            at = unpack(block, pair, at)
    for block, target in ((query, gq), (key, gk), (value, gv)):
        send(block, target)
    for copy in outs:
        copy.wait()


ANY = pl.BlockSpec(memory_space=pl.ANY)
WHOLE = pl.BlockSpec(memory_space=pltpu.VMEM)


def per_device(
    dp_size, molecules, gain_attn, w_query, w_key, w_value, w_output, gain_ffn, w_inner, w_outer, cotangent, span_mask
):
    count, shard, width = molecules.shape
    heads_width = w_query.shape[1]
    units_inner = w_inner.shape[1]
    rows = 2 * count * shard
    extra = (dp_size // 16).bit_length() - 1
    levels = 5 + extra
    act, gmol, sums, gains = pl.pallas_call(
        functools.partial(layer_kernel, dp_size),
        out_shape=(
            pltpu.VMEM(molecules.shape, bf16),
            pltpu.VMEM(molecules.shape, f32),
            pltpu.VMEM((UNITS, ROWS, 128), bf16),
            pltpu.VMEM((8, width), f32),
        ),
        in_specs=[ANY] * 10 + [WHOLE],
        out_specs=(WHOLE, WHOLE, WHOLE, WHOLE),
        scratch_shapes=[
            pltpu.VMEM((8, width), f32),
            pltpu.VMEM(molecules.shape, bf16),
            pltpu.VMEM(molecules.shape, bf16),
            pltpu.VMEM((width, 3 * heads_width), bf16),
            pltpu.VMEM(w_output.shape, bf16),
            pltpu.VMEM(w_inner.shape, bf16),
            pltpu.VMEM(w_outer.shape, bf16),
            pltpu.VMEM((rows, width), bf16),
            pltpu.VMEM((width, rows), bf16),
            pltpu.VMEM((rows, 3 * heads_width), bf16),
            pltpu.VMEM((rows, heads_width), bf16),
            pltpu.VMEM((heads_width, rows), bf16),
            pltpu.VMEM((3,) + molecules.shape, bf16),
            pltpu.VMEM((2,) + molecules.shape, bf16),
            pltpu.VMEM((rows, width), bf16),
            pltpu.VMEM((rows, width), bf16),
            pltpu.VMEM((rows, units_inner), bf16),
            pltpu.VMEM((rows, units_inner), bf16),
            pltpu.VMEM((count, rows // 2, 128), f32),
            pltpu.VMEM(molecules.shape, f32),
            pltpu.VMEM((levels, 8, width), f32),
            pltpu.VMEM((levels, 8, width), f32),
            pltpu.VMEM((UNITS, ROWS, 128), bf16),
            pltpu.VMEM((UNITS, 2, QUAD, 128), bf16),
            pltpu.VMEM((UNITS, 2, QUAD, 128), bf16),
            pltpu.VMEM((UNITS, 2, PART, 128), bf16),
            pltpu.VMEM((UNITS if extra else 1, 2, max(extra, 1), PART, 128), bf16),
            pltpu.SemaphoreType.DMA((17,)),
            pltpu.SemaphoreType.DMA((16,)),
            pltpu.SemaphoreType.DMA((16,)),
            pltpu.SemaphoreType.DMA((levels,)),
            pltpu.SemaphoreType.DMA((levels,)),
            pltpu.SemaphoreType.DMA((6 + 2 * extra,)),
            pltpu.SemaphoreType.DMA((UNITS, 6 + 2 * extra)),
            pltpu.SemaphoreType.DMA((1,)),
        ],
        compiler_params=pltpu.CompilerParams(
            collective_id=0, has_side_effects=True, vmem_limit_bytes=VMEM_LIMIT),
        name="layer",
    )(
        molecules, gain_attn, w_query, w_key, w_value, w_output, gain_ffn,
        w_inner, w_outer, cotangent, span_mask,
    )
    shapes = [jax.ShapeDtypeStruct(w.shape, f32) for w in (w_query, w_key, w_value, w_output, w_inner, w_outer)]
    outs = pl.pallas_call(
        finish_kernel,
        out_shape=(
            jax.ShapeDtypeStruct(molecules.shape, bf16), jax.ShapeDtypeStruct(molecules.shape, f32), *shapes,
            jax.ShapeDtypeStruct((width,), f32), jax.ShapeDtypeStruct((width,), f32)),
        in_specs=[WHOLE] * 4,
        out_specs=(ANY,) * 10,
        scratch_shapes=[pltpu.VMEM(shape.shape, f32) for shape in shapes]
        + [pltpu.SemaphoreType.DMA((4 + FF_UNITS + 4,))],
        compiler_params=pltpu.CompilerParams(vmem_limit_bytes=40 * 2 ** 20),
        name="finish",
    )(act, gmol, sums, gains)
    return tuple(outs)


def solution(mesh):
    in_specs = (
        P("dp", "mp", None),
        P(),
        P(None, "mp"),
        P(None, "mp"),
        P(None, "mp"),
        P("mp", None),
        P(),
        P(None, "mp"),
        P("mp", None),
        P("dp", "mp", None),
        P("dp", "mp"),
    )
    out_specs = (
        P("dp", "mp", None),
        P("dp", "mp", None),
        P(None, "mp"),
        P(None, "mp"),
        P(None, "mp"),
        P("mp", None),
        P(None, "mp"),
        P("mp", None),
        P(),
        P(),
    )
    return jax.shard_map(
        functools.partial(per_device, mesh.shape["dp"]),
        mesh=mesh, in_specs=in_specs, out_specs=out_specs, check_vma=False,
    )
```

```python
import functools

import jax
import jax.numpy as jnp
from jax import lax
from jax.experimental import pallas as pl
from jax.experimental.pallas import tpu as pltpu
from jax.sharding import PartitionSpec as P

HEAD_DIM = 64
EPSILON = 1e-05
MESH = pl.DeviceIdType.MESH
bf16 = jnp.bfloat16
f32 = jnp.float32

ROWS = 1536
HALF = ROWS // 2
QUAD = HALF // 2
SIDE = QUAD // 2
PART = SIDE // 2
FF_UNITS = 12
UNITS = 18
BLOCK = 256
GAIN_SPACING = 10


VMEM_LIMIT = 54 * 2 ** 20

SCHEDULE = (
    ((0, 0),),
    ((0, 1),),
    ((0, 2),),
    ((0, 3), (1, 0),),
    ((0, 4), (1, 1),),
    ((0, 5),),
    ((1, 3), (1, 2), (0, 7), (2, 0),),
    ((2, 1), (1, 4), (0, 9),),
    ((1, 5), (2, 3), (0, 11), (3, 0),),
    ((1, 7), (3, 1), (2, 2),),
    ((4, 0), (2, 5), (2, 4), (3, 3), (1, 11), (1, 9),),
    ((0, 6), (3, 2),),
    ((4, 1), (5, 0), (2, 7),),
    ((0, 8), (3, 5), (2, 11),),
    ((1, 6), (0, 10), (4, 3), (3, 4), (2, 9),),
    ((6, 0), (4, 2), (5, 1),),
    ((0, 12), (1, 8), (3, 7),),
    ((1, 10), (4, 5), (4, 4), (7, 0), (5, 3), (3, 11), (2, 6), (3, 9), (5, 2),),
    ((2, 8), (1, 12), (6, 1), (4, 7), (5, 5),),
    ((0, 13), (0, 14), (5, 4), (6, 2), (2, 10), (6, 3), (8, 0),),
    ((4, 11), (2, 12), (4, 9), (3, 6), (6, 5), (5, 7),),
    ((3, 8), (1, 13), (3, 10), (7, 2), (9, 0), (1, 14), (7, 1),),
    ((0, 15), (6, 4), (5, 11), (5, 9), (3, 12), (7, 3),),
    ((4, 6), (8, 2), (6, 7), (7, 5), (10, 0),),
    ((1, 15), (4, 8), (6, 9), (4, 10), (2, 13), (8, 1), (6, 11),),
    ((2, 14), (0, 16), (0, 17), (4, 12), (5, 6), (8, 3),),
    ((7, 4), (8, 5), (5, 8), (5, 10), (9, 2),),
    ((7, 7), (3, 13),),
    ((1, 16), (3, 14), (9, 1), (2, 15),),
    ((1, 17), (9, 3), (6, 6), (7, 9), (5, 12), (6, 8), (8, 4),),
    ((9, 5), (7, 11), (6, 10), (4, 13), (8, 7), (10, 2), (2, 16), (3, 15), (4, 14), (10, 1), (2, 17), (8, 9),
     (7, 6), (8, 11), (7, 8), (3, 16), (7, 10), (3, 17), (9, 4), (10, 3), (6, 12), (9, 7), (10, 5), (5, 13),
     (5, 14), (4, 15), (10, 4), (9, 9), (10, 7), (9, 11), (6, 13), (6, 14), (5, 15), (4, 16), (10, 9), (4, 17),
     (10, 11), (6, 15), (5, 16), (5, 17), (7, 12), (8, 6), (9, 6), (6, 16), (6, 17), (8, 8), (9, 8), (7, 13),
     (8, 10), (9, 10), (10, 6), (7, 14), (8, 12), (9, 12), (10, 8), (8, 13), (7, 15), (8, 14), (9, 13), (10, 10),
     (9, 14), (10, 12), (7, 16), (8, 15), (7, 17), (9, 15), (10, 13), (8, 16), (9, 16), (10, 14), (8, 17), (9, 17),
     (10, 15), (10, 16), (10, 17),),
)


def al(v, m):
    return pl.multiple_of(v, m)


class Ring:
    def __init__(self, grads, far, line, near, beyond, out, send_sem, recv_sem, own_sem, dp_size):
        self.grads, self.far, self.line, self.near, self.beyond, self.out = grads, far, line, near, beyond, out
        self.send_sem, self.recv_sem, self.own_sem = send_sem, recv_sem, own_sem
        self.extra = (dp_size // 16).bit_length() - 1
        self.dp = lax.axis_index("dp")
        self.mp = lax.axis_index("mp")
        place = lax.rem(lax.div(self.dp, 4), 4)
        low = jnp.where(place < 2, 1, 0)
        self.is_end = (place == 0) | (place == 3)
        self.is_mid = (place == 1) | (place == 2)
        self.inward = self.dp + 4 * (2 * low - 1)
        self.outward = self.dp - 4 * (2 * low - 1)
        self.far_side = low * SIDE
        self.own_side = (1 - low) * SIDE
        bits = (lax.rem(self.dp, 2), lax.rem(lax.div(self.dp, 2), 2))
        self.first_bit = bits
        self.last_bit = (bits[1], bits[0])
        self.first_peer = [self.dp + (1 - 2 * bits[h]) * (1 << h) for h in range(2)]
        self.last_peer = [self.first_peer[1], self.first_peer[0]]

    def kept(self, h, offset, count):
        return pl.ds(al(h * HALF + self.first_bit[h] * QUAD + offset, 16), count)

    def side(self, offset, count=SIDE):
        return pl.ds(al(offset, 16), count)

    def copy(self, src, dst, u, sent, received, dp):
        return pltpu.make_async_remote_copy(
            src_ref=src, dst_ref=dst, send_sem=self.send_sem.at[sent], recv_sem=self.recv_sem.at[u, received],
            device_id=(dp, self.mp), device_id_type=MESH)

    def received(self, block, u, k):
        self.copy(block, block, u, k, k, self.first_peer[0]).wait_recv()

    def was_sent(self, block, k):
        self.copy(block, block, 0, k, 0, self.first_peer[0]).wait_send()

    def add(self, u, rows, other):
        self.grads[u, rows] = (self.grads[u, rows].astype(f32) + other.astype(f32)).astype(bf16)

    def pass_sum(self, u, offset, sent, received, dp):
        for h in range(2):
            self.copy(self.grads.at[u, self.kept(h, offset, SIDE)], self.line.at[u, h, self.side(offset)],
                      u, sent, received, dp).start()

    def take_sum(self, u, offset, received):
        self.received(self.line.at[u, :, self.side(offset)], u, received)
        for h in range(2):
            self.add(u, self.kept(h, offset, SIDE), self.line[u, h, self.side(offset)])

    def pass_whole(self, u, offset, sent, received, dp):
        for h in range(2):
            block = self.far.at[u, h, self.side(offset)]
            self.copy(block, block, u, sent, received, dp).start()

    def take_whole(self, u, offset, received):
        self.received(self.far.at[u, :, self.side(offset)], u, received)

    def finish(self, u):
        for h in range(2):
            rows = self.kept(h, 0, QUAD)
            self.copy(self.far.at[u, h], self.out.at[u, rows], u, 5, 5, self.first_peer[h]).start()
            pltpu.make_async_copy(self.far.at[u, h], self.out.at[u, rows], self.own_sem.at[0]).start()

    def stage0(self, u):
        for h in range(2):
            rows = pl.ds(al(h * HALF + (1 - self.first_bit[h]) * QUAD, 16), QUAD)
            self.copy(self.grads.at[u, rows], self.far.at[u, h], u, 0, 0, self.first_peer[h]).start()

    def stage1(self, u):
        self.received(self.far.at[u], u, 0)
        for h in range(2):
            self.add(u, self.kept(h, 0, QUAD), self.far[u, h])

        @pl.when(self.is_end)
        def _():
            self.pass_sum(u, self.far_side, 1, 1, self.inward)

    def stage2(self, u):
        @pl.when(self.is_mid)
        def _():
            self.take_sum(u, self.far_side, 1)
            self.pass_sum(u, self.far_side, 1, 2, self.inward)

    def stage3(self, u):
        @pl.when(self.is_mid)
        def _():
            self.take_sum(u, self.own_side, 2)
            self.pass_sum(u, self.own_side, 2, 2, self.outward)

    def stage4(self, u):
        @pl.when(self.is_end)
        def _():
            self.take_sum(u, self.own_side, 2)
            for h in range(2):
                rows = self.kept(h, self.own_side + (1 - self.last_bit[h]) * PART, PART)
                self.copy(self.grads.at[u, rows], self.near.at[u, h], u, 2, 1, self.last_peer[h]).start()

    def stage5(self, u):
        @pl.when(self.is_end)
        def _():
            self.received(self.near.at[u], u, 1)
            for h in range(2):
                offset = self.own_side + self.last_bit[h] * PART
                mine = self.kept(h, offset, PART)
                last = self.near[u, h]
                for k in range(self.extra):
                    self.add(u, mine, last)
                    copy = self.copy(self.grads.at[u, mine], self.beyond.at[u, h, k], u, 6 + 2 * k + h, 6 + 2 * k + h,
                                     self.dp ^ (16 << k))
                    copy.start()
                    copy.wait()
                    last = self.beyond[u, h, k]
                rows = self.side(offset, PART)
                self.far[u, h, rows] = (self.grads[u, mine].astype(f32) + last.astype(f32)).astype(bf16)
                block = self.far.at[u, h, rows]
                self.copy(block, block, u, 3, 3, self.last_peer[h]).start()

    def stage6(self, u):
        @pl.when(self.is_end)
        def _():
            self.received(self.near.at[u], u, 3)
            self.pass_whole(u, self.own_side, 4, 3, self.inward)

    def stage7(self, u):
        @pl.when(self.is_mid)
        def _():
            self.take_whole(u, self.own_side, 3)
            self.pass_whole(u, self.own_side, 3, 4, self.inward)

    def stage8(self, u):
        @pl.when(self.is_mid)
        def _():
            self.take_whole(u, self.far_side, 4)
            self.pass_whole(u, self.far_side, 4, 4, self.outward)
            self.finish(u)

    def stage9(self, u):
        @pl.when(self.is_end)
        def _():
            self.take_whole(u, self.far_side, 4)
            self.finish(u)

    def stage10(self, u):
        self.received(self.far.at[u], u, 5)

    def sent(self):
        self.was_sent(self.far, 0)
        self.was_sent(self.far, 5)
        pltpu.make_async_copy(self.far, self.far, self.own_sem.at[0]).wait()
        one_side = self.line.at[:, :, pl.ds(0, SIDE)]

        @pl.when(self.is_end)
        def _():
            for k, block in ((1, one_side), (2, self.near), (3, self.near), (4, one_side)):
                self.was_sent(block, k)

        @pl.when(self.is_mid)
        def _():
            for k in range(1, 5):
                self.was_sent(one_side, k)

    def stages(self):
        return (self.stage0, self.stage1, self.stage2, self.stage3, self.stage4, self.stage5, self.stage6,
                self.stage7, self.stage8, self.stage9, self.stage10)


def dot(a, b):
    return jnp.dot(a, b, preferred_element_type=f32)


def dot_nt(a, b):
    return lax.dot_general(a, b, (((1,), (1,)), ((), ())), preferred_element_type=f32)


def normalize(values):
    centred = values - jnp.mean(values, axis=-1, keepdims=True)
    inv_std = lax.rsqrt(jnp.mean(centred * centred, axis=-1, keepdims=True) + EPSILON)
    return centred * inv_std, inv_std


def norm_back(grad, scaled, inv_std, gain):
    grad_scaled = grad * gain
    mean_first = jnp.mean(grad_scaled, axis=-1, keepdims=True)
    mean_second = jnp.mean(grad_scaled * scaled, axis=-1, keepdims=True)
    return inv_std * (grad_scaled - mean_first - scaled * mean_second), jnp.sum(grad * scaled, axis=0, keepdims=True)


def layer_kernel(
    dp_size, mol_hbm, gain_one_hbm, wq_hbm, wk_hbm, wv_hbm, wo_hbm, gain_two_hbm, wi_hbm, wu_hbm, cot_hbm, mask_ref,
    act_out, gmol_out, sums_out, gains_out,
    gains, x, cot, wqkv, wo, wi, wu, n1, turned, qkv, mixed, mixed_t, pin, pout, n2, gres, act, gip, lse, hid,
    gains_sum, gains_in, grads, far, line, near, beyond,
    in_sem, mp_send, mp_recv, gain_send, gain_recv, ring_send, ring_recv, ring_own,
):
    mp = lax.axis_index("mp")
    dp = lax.axis_index("dp")
    rows, width = n1.shape
    half = rows // 2
    shard = half // 2
    heads_width = wo.shape[0]
    pairs = heads_width // 128
    joined = 3 * 128
    ring = Ring(grads, far, line, near, beyond, sums_out, ring_send, ring_recv, ring_own, dp_size)
    stages = ring.stages()
    own = pl.ds(al(mp * half, half), half)
    other = pl.ds(al((1 - mp) * half, half), half)
    gbr = n2
    slot = iter(SCHEDULE)

    def advance():
        for stage, unit in next(slot, ()):
            stages[stage](unit)

    def own_of(s):
        return pl.ds(al(mp * half + s * shard, shard), shard)

    def other_of(s):
        return pl.ds(al((1 - mp) * half + s * shard, shard), shard)

    def take(ref, s, columns):
        return jnp.concatenate([ref[pl.ds(s * shard, shard), columns], ref[pl.ds(half + s * shard, shard), columns]])

    def put(ref, s, columns, values):
        ref[pl.ds(s * shard, shard), columns] = values[:shard]
        ref[pl.ds(half + s * shard, shard), columns] = values[shard:]

    def to_peer(src, dst, k):
        return pltpu.make_async_remote_copy(
            src_ref=src, dst_ref=dst, send_sem=mp_send.at[k], recv_sem=mp_recv.at[k],
            device_id=(dp, 1 - mp), device_id_type=MESH)

    def rows_copy(ref, s, k):
        return to_peer(ref.at[own_of(s)], ref.at[own_of(s)], k)

    def part_copy(kind, s):
        return to_peer(pout.at[kind % 2, s], pin.at[kind % 3, s], 8 + 2 * kind + s)

    def whole_part(kind):
        return to_peer(pout.at[kind % 2], pin.at[kind % 3], 8 + 2 * kind)

    gain_one = gains.at[pl.ds(0, 1)]
    gain_two = gains.at[pl.ds(1, 1)]

    loads = [
        pltpu.make_async_copy(mol_hbm.at[0], x.at[0], in_sem.at[0]),
        pltpu.make_async_copy(mol_hbm.at[1], x.at[1], in_sem.at[1]),
    ]
    for kind, source in enumerate((wq_hbm, wk_hbm, wv_hbm)):
        for pair in range(pairs):
            loads.append(pltpu.make_async_copy(
                source.at[:, pl.ds(pair * 128, 128)], wqkv.at[:, pl.ds(pair * joined + kind * 128, 128)],
                in_sem.at[len(loads)]))
    weights = loads[2:]
    others = []
    for source, target in ((cot_hbm, cot), (wo_hbm, wo), (wi_hbm, wi), (wu_hbm, wu)):
        others.append(pltpu.make_async_copy(source, target, in_sem.at[len(loads) + len(others)]))
    gain_loads = [
        pltpu.make_async_copy(source, gains.at[k], in_sem.at[len(loads) + len(others) + k])
        for k, source in enumerate((gain_one_hbm, gain_two_hbm))
    ]
    for load in gain_loads + loads + others:
        load.start()

    barrier = pltpu.get_barrier_semaphore()
    flips = [1, 2, 4, 8, 12] + [16 << k for k in range(ring.extra)]
    for flip in flips:
        pl.semaphore_signal(barrier, inc=1, device_id=(dp ^ flip, mp), device_id_type=MESH)
    pl.semaphore_signal(barrier, inc=1, device_id=(dp, 1 - mp), device_id_type=MESH)

    for load in gain_loads:
        load.wait()
    for s in range(2):
        loads[s].wait()
        scaled, _ = normalize(x[s].astype(f32))
        n1[own_of(s), :] = (scaled * gain_one[...]).astype(bf16)
        if s == 0:
            pl.semaphore_wait(barrier, len(flips) + 1)
        rows_copy(n1, s, s).start()

    others[0].wait()
    lanes = lax.broadcasted_iota(jnp.int32, (128, 128), 1)
    subs = lax.broadcasted_iota(jnp.int32, (128, 128), 0)
    for s in range(2):
        for piece in range(shard // 128):
            row = mask_ref[pl.ds(s, 1), pl.ds(piece * 128, 128)].astype(f32)
            column = jnp.sum(jnp.where(lanes == subs, row, 0.0), axis=1, keepdims=True)
            weight = 0.25 + 0.75 * column
            values = cot[s, pl.ds(piece * 128, 128), :].astype(f32) * weight
            gres[pl.ds(al(mp * half + s * shard + piece * 128, 128), 128), :] = values.astype(bf16)
        rows_copy(gres, s, 2 + s).start()

    lane = lax.broadcasted_iota(jnp.int32, (1, 128), 1)
    sides = (lane < HEAD_DIM, lane >= HEAD_DIM)
    scale = HEAD_DIM ** -0.5

    def columns(pair, kind):
        return pl.ds(pair * joined + kind * 128, 128)

    for load in weights:
        load.wait()
    qkv[own, :] = dot(n1[own, :], wqkv[...]).astype(bf16)
    for s in range(2):
        rows_copy(n1, s, s).wait_recv()
    qkv[other, :] = dot(n1[other, :], wqkv[...]).astype(bf16)
    others[1].wait()

    def second_norm(s):
        part_copy(0, s).wait_recv()
        hidden = hid[s] + pin[0, s].astype(f32)
        hid[s] = hidden
        scaled, _ = normalize(hidden)
        n2[own_of(s), :] = (scaled * gain_two[...]).astype(bf16)
        rows_copy(n2, s, 4 + s).start()

    for s in range(2):
        logs = jnp.zeros((half, 128), f32)
        for pair in range(pairs):
            query = take(qkv, s, columns(pair, 0)) * jnp.asarray(scale, bf16)
            key = take(qkv, s, columns(pair, 1))
            value = take(qkv, s, columns(pair, 2))
            outs = []
            for side in range(2):
                scores = dot_nt(jnp.where(sides[side], query, 0), key)
                row_max = jnp.max(scores, axis=-1, keepdims=True)
                expon = jnp.exp(scores - row_max)
                total = jnp.sum(expon, axis=-1, keepdims=True)
                logs = jnp.where(lane == 2 * pair + side, row_max + jnp.log(total), logs)
                outs.append(dot(expon.astype(bf16), value) * (1.0 / total))
            put(mixed, s, pl.ds(pair * 128, 128), jnp.where(sides[0], outs[0], outs[1]).astype(bf16))
            if s == 1 and pair == 1:
                second_norm(0)
        lse[s] = logs
        pout[0, s] = dot(mixed[other_of(s), :], wo[...]).astype(bf16)
        part_copy(0, s).start()
        hid[s] = x[s].astype(f32) + dot(mixed[own_of(s), :], wo[...])
    second_norm(1)
    mixed_t[...] = mixed[...].T
    turned[:, own] = n2[own, :].T
    for s in range(2):
        rows_copy(gres, s, 2 + s).wait_recv()
    others[2].wait()
    others[3].wait()
    for s in range(2):
        rows_copy(n2, s, 4 + s).wait_recv()
    turned[:, other] = n2[other, :].T

    def grad_outer(b):
        part = dot(act[:, pl.ds(b * BLOCK, BLOCK)].T, gres[...]).astype(bf16)
        for g in range(width // 128):
            grads[2 * b, pl.ds(g * BLOCK, BLOCK), :] = part[:, g * 128:(g + 1) * 128]
        advance()

    blocks = wi.shape[1] // BLOCK
    for b in range(blocks):
        block = pl.ds(b * BLOCK, BLOCK)
        inner = dot(n2[...], wi[:, block])
        shape = 1.0 + lax.erf(inner * (0.5 ** 0.5))
        act[:, block] = (0.5 * inner * shape).astype(bf16)
        slope = 0.5 * shape + inner * (jnp.exp(-0.5 * inner * inner) * (2.0 * 3.141592653589793) ** -0.5)
        if b < blocks // 2:
            grad_outer(b)
        back = dot_nt(gres[...], wu[block, :])
        pre = (back * slope).astype(bf16)
        gip[:, block] = pre
        part = dot(turned[...], pre).astype(bf16)
        for g in range(BLOCK // 128):
            grads[2 * b + 1, pl.ds(g * width, width), :] = part[:, g * 128:(g + 1) * 128]
        advance()

    def send_part(kind, values):
        if kind >= 2:
            for s in range(2 if kind == 2 else 0):
                part_copy(0, s).wait_send()
            if kind == 3:
                whole_part(1).wait_send()
        for s in range(2):
            pout[kind % 2, s] = values[s * shard:(s + 1) * shard].astype(bf16)
        whole_part(kind).start()

    send_part(1, dot_nt(gip[other, :], wi[...]))
    advance()
    grad = dot_nt(gip[own, :], wi[...])
    turned[...] = n1[...].T
    advance()
    grad_outer(blocks // 2)
    whole_part(1).wait_recv()
    gain_two_sum = jnp.zeros((1, width), f32)
    for s in range(2):
        scaled, inv_std = normalize(hid[s])
        grad_values, gain_part = norm_back(
            grad[s * shard:(s + 1) * shard] + pin[1, s].astype(f32), scaled, inv_std, gain_two[...])
        gain_two_sum += gain_part
        grad_hidden = gres[own_of(s), :].astype(f32) + grad_values
        gbr_rows = grad_hidden.astype(bf16)
        if s == 0:
            for k in range(2):
                rows_copy(n2, k, 4 + k).wait_send()
        gmol_out[s] = grad_hidden
        gbr[own_of(s), :] = gbr_rows
        rows_copy(gbr, s, 6 + s).start()
    advance()
    for b in range(blocks // 2 + 1, blocks):
        grad_outer(b)
    for s in range(2):
        rows_copy(gbr, s, 6 + s).wait_recv()
    mixed[...] = dot_nt(gbr[...], wo[...]).astype(bf16)
    advance()
    part = dot(mixed_t[...], gbr[...]).astype(bf16)
    for g in range(width // 128):
        at = g * heads_width
        grads[FF_UNITS + at // ROWS, pl.ds(at % ROWS, heads_width), :] = part[:, g * 128:(g + 1) * 128]
    advance()

    for pair in range(pairs):
        for s in range(2):
            query = take(qkv, s, columns(pair, 0)) * jnp.asarray(scale, bf16)
            key = take(qkv, s, columns(pair, 1))
            value = take(qkv, s, columns(pair, 2))
            grad_mixed = take(mixed, s, pl.ds(pair * 128, 128))
            logs = lse[s]
            query_t = query.T
            grad_mixed_t = grad_mixed.T
            found = []
            for side in range(2):
                log_total = jnp.sum(jnp.where(lane == 2 * pair + side, logs, 0.0), axis=-1, keepdims=True)
                probs = jnp.exp(dot_nt(jnp.where(sides[side], query, 0), key) - log_total)
                grad_probs = dot_nt(jnp.where(sides[side], grad_mixed, 0), value)
                row_inner = jnp.sum(probs * grad_probs, axis=-1, keepdims=True)
                grad_scores = (probs * (grad_probs - row_inner)).astype(bf16)
                grad_value = dot(grad_mixed_t, probs.astype(bf16))
                grad_query = dot(grad_scores, key) * scale
                grad_key = dot(query_t, grad_scores)
                found.append((grad_query, grad_key, grad_value))
            put(gip, s, columns(pair, 0), jnp.where(sides[0], found[0][0], found[1][0]).astype(bf16))
            for kind in (1, 2):
                joint = jnp.concatenate([found[0][kind][:HEAD_DIM], found[1][kind][HEAD_DIM:]])
                put(gip, s, columns(pair, kind), joint.astype(bf16).T)
            advance()
        part = dot(turned[...], gip[:, pl.ds(pair * joined, joined)]).astype(bf16)
        for kind in range(3):
            at = width // 128 * heads_width + (pair * 3 + kind) * width
            grads[FF_UNITS + at // ROWS, pl.ds(at % ROWS, width), :] = part[:, kind * 128:(kind + 1) * 128]
        advance()

    all_joined = pl.ds(0, pairs * joined)
    send_part(3, dot_nt(gip[other, all_joined], wqkv[...]))
    advance()
    grad = dot_nt(gip[own, all_joined], wqkv[...])
    advance()
    send_part(2, dot(act[other, :], wu[...]))
    advance()
    result = dot(act[own, :], wu[...])
    whole_part(2).wait_recv()
    for s in range(2):
        act_out[s] = (hid[s] + result[s * shard:(s + 1) * shard] + pin[2, s].astype(f32)).astype(bf16)
    advance()
    whole_part(3).wait_recv()
    gain_one_sum = jnp.zeros((1, width), f32)
    for s in range(2):
        scaled, inv_std = normalize(x[s].astype(f32))
        grad_values, gain_part = norm_back(
            grad[s * shard:(s + 1) * shard] + pin[0, s].astype(f32), scaled, inv_std, gain_one[...])
        gain_one_sum += gain_part
        gmol_out[s] = gmol_out[s] + grad_values
    gains_sum[0] = jnp.zeros(gains_sum.shape[1:], f32)
    gains_sum[0, pl.ds(0, 1), :] = gain_one_sum
    gains_sum[0, pl.ds(1, 1), :] = gain_two_sum

    targets = [(dp, 1 - mp)] + [(dp ^ (1 << k), mp) for k in range(4 + ring.extra)]

    def gain_copy(k):
        return pltpu.make_async_remote_copy(
            src_ref=gains_sum.at[k], dst_ref=gains_in.at[k], send_sem=gain_send.at[k], recv_sem=gain_recv.at[k],
            device_id=targets[k], device_id_type=MESH)

    def gain_step(k):
        if k:
            gain_copy(k - 1).wait_recv()
            total = gains_sum[k - 1] + gains_in[k - 1]
            if k == len(targets):
                gains_out[...] = total
            else:
                gains_sum[k] = total
        if k < len(targets):
            gain_copy(k).start()

    tail = [step for part in slot for step in part]
    steps = len(targets) + 1
    for i, (stage, unit) in enumerate(tail):
        if i % GAIN_SPACING == 0 and i // GAIN_SPACING < steps:
            gain_step(i // GAIN_SPACING)
        stages[stage](unit)
    for k in range(-(-len(tail) // GAIN_SPACING), steps):
        gain_step(k)

    for s in range(2):
        rows_copy(n1, s, s).wait_send()
        rows_copy(gres, s, 2 + s).wait_send()
        rows_copy(gbr, s, 6 + s).wait_send()
    for kind in (2, 3):
        whole_part(kind).wait_send()
    for k in range(len(targets)):
        gain_copy(k).wait_send()
    ring.sent()


def finish_kernel(
    act_in, gmol_in, packed, gains_in, act_out, gmol_out, gq, gk, gv, go, gi, gu, gain_one_out, gain_two_out,
    query, key, value, output, inner, outer, out_sem,
):
    width, heads_width = query.shape
    outs = []

    def send(src, dst):
        copy = pltpu.make_async_copy(src, dst, out_sem.at[len(outs)])
        copy.start()
        outs.append(copy)
    send(act_in, act_out)
    send(gmol_in, gmol_out)
    send(gains_in.at[0], gain_one_out)
    send(gains_in.at[1], gain_two_out)
    for b in range(FF_UNITS // 2):
        for g in range(width // 128):
            outer[pl.ds(b * BLOCK, BLOCK), pl.ds(g * 128, 128)] = packed[2 * b, pl.ds(g * BLOCK, BLOCK), :].astype(f32)
        send(outer.at[pl.ds(b * BLOCK, BLOCK)], gu.at[pl.ds(b * BLOCK, BLOCK)])
        for g in range(BLOCK // 128):
            inner[:, pl.ds(b * BLOCK + g * 128, 128)] = packed[2 * b + 1, pl.ds(g * width, width), :].astype(f32)
        send(inner.at[:, pl.ds(b * BLOCK, BLOCK)], gi.at[:, pl.ds(b * BLOCK, BLOCK)])
    at = FF_UNITS * ROWS

    def unpack(block, g, at):
        count = block.shape[0]
        block[:, pl.ds(g * 128, 128)] = packed[at // ROWS, pl.ds(at % ROWS, count), :].astype(f32)
        return at + count
    for g in range(width // 128):
        at = unpack(output, g, at)
    send(output, go)
    for pair in range(heads_width // 128):
        for block in (query, key, value):
            at = unpack(block, pair, at)
    for block, target in ((query, gq), (key, gk), (value, gv)):
        send(block, target)
    for copy in outs:
        copy.wait()


ANY = pl.BlockSpec(memory_space=pl.ANY)
WHOLE = pl.BlockSpec(memory_space=pltpu.VMEM)


def per_device(
    dp_size, molecules, gain_attn, w_query, w_key, w_value, w_output, gain_ffn, w_inner, w_outer, cotangent, span_mask
):
    count, shard, width = molecules.shape
    heads_width = w_query.shape[1]
    units_inner = w_inner.shape[1]
    rows = 2 * count * shard
    extra = (dp_size // 16).bit_length() - 1
    levels = 5 + extra
    act, gmol, sums, gains = pl.pallas_call(
        functools.partial(layer_kernel, dp_size),
        out_shape=(
            pltpu.VMEM(molecules.shape, bf16),
            pltpu.VMEM(molecules.shape, f32),
            pltpu.VMEM((UNITS, ROWS, 128), bf16),
            pltpu.VMEM((8, width), f32),
        ),
        in_specs=[ANY] * 10 + [WHOLE],
        out_specs=(WHOLE, WHOLE, WHOLE, WHOLE),
        scratch_shapes=[
            pltpu.VMEM((8, width), f32),
            pltpu.VMEM(molecules.shape, bf16),
            pltpu.VMEM(molecules.shape, bf16),
            pltpu.VMEM((width, 3 * heads_width), bf16),
            pltpu.VMEM(w_output.shape, bf16),
            pltpu.VMEM(w_inner.shape, bf16),
            pltpu.VMEM(w_outer.shape, bf16),
            pltpu.VMEM((rows, width), bf16),
            pltpu.VMEM((width, rows), bf16),
            pltpu.VMEM((rows, 3 * heads_width), bf16),
            pltpu.VMEM((rows, heads_width), bf16),
            pltpu.VMEM((heads_width, rows), bf16),
            pltpu.VMEM((3,) + molecules.shape, bf16),
            pltpu.VMEM((2,) + molecules.shape, bf16),
            pltpu.VMEM((rows, width), bf16),
            pltpu.VMEM((rows, width), bf16),
            pltpu.VMEM((rows, units_inner), bf16),
            pltpu.VMEM((rows, units_inner), bf16),
            pltpu.VMEM((count, rows // 2, 128), f32),
            pltpu.VMEM(molecules.shape, f32),
            pltpu.VMEM((levels, 8, width), f32),
            pltpu.VMEM((levels, 8, width), f32),
            pltpu.VMEM((UNITS, ROWS, 128), bf16),
            pltpu.VMEM((UNITS, 2, QUAD, 128), bf16),
            pltpu.VMEM((UNITS, 2, QUAD, 128), bf16),
            pltpu.VMEM((UNITS, 2, PART, 128), bf16),
            pltpu.VMEM((UNITS if extra else 1, 2, max(extra, 1), PART, 128), bf16),
            pltpu.SemaphoreType.DMA((17,)),
            pltpu.SemaphoreType.DMA((16,)),
            pltpu.SemaphoreType.DMA((16,)),
            pltpu.SemaphoreType.DMA((levels,)),
            pltpu.SemaphoreType.DMA((levels,)),
            pltpu.SemaphoreType.DMA((6 + 2 * extra,)),
            pltpu.SemaphoreType.DMA((UNITS, 6 + 2 * extra)),
            pltpu.SemaphoreType.DMA((1,)),
        ],
        compiler_params=pltpu.CompilerParams(
            collective_id=0, has_side_effects=True, vmem_limit_bytes=VMEM_LIMIT),
        name="layer",
    )(
        molecules, gain_attn, w_query, w_key, w_value, w_output, gain_ffn,
        w_inner, w_outer, cotangent, span_mask,
    )
    shapes = [jax.ShapeDtypeStruct(w.shape, f32) for w in (w_query, w_key, w_value, w_output, w_inner, w_outer)]
    outs = pl.pallas_call(
        finish_kernel,
        out_shape=(
            jax.ShapeDtypeStruct(molecules.shape, bf16), jax.ShapeDtypeStruct(molecules.shape, f32), *shapes,
            jax.ShapeDtypeStruct((width,), f32), jax.ShapeDtypeStruct((width,), f32)),
        in_specs=[WHOLE] * 4,
        out_specs=(ANY,) * 10,
        scratch_shapes=[pltpu.VMEM(shape.shape, f32) for shape in shapes]
        + [pltpu.SemaphoreType.DMA((4 + FF_UNITS + 4,))],
        compiler_params=pltpu.CompilerParams(vmem_limit_bytes=40 * 2 ** 20),
        name="finish",
    )(act, gmol, sums, gains)
    return tuple(outs)


def solution(mesh):
    in_specs = (
        P("dp", "mp", None),
        P(),
        P(None, "mp"),
        P(None, "mp"),
        P(None, "mp"),
        P("mp", None),
        P(),
        P(None, "mp"),
        P("mp", None),
        P("dp", "mp", None),
        P("dp", "mp"),
    )
    out_specs = (
        P("dp", "mp", None),
        P("dp", "mp", None),
        P(None, "mp"),
        P(None, "mp"),
        P(None, "mp"),
        P("mp", None),
        P(None, "mp"),
        P("mp", None),
        P(),
        P(),
    )
    return jax.shard_map(
        functools.partial(per_device, mesh.shape["dp"]),
        mesh=mesh, in_specs=in_specs, out_specs=out_specs, check_vma=False,
    )
```

```python
import functools

import jax
import jax.numpy as jnp
from jax import lax
from jax.experimental import pallas as pl
from jax.experimental.pallas import tpu as pltpu
from jax.sharding import PartitionSpec as P

HEAD_DIM = 64
EPSILON = 1e-05
MESH = pl.DeviceIdType.MESH
bf16 = jnp.bfloat16
f32 = jnp.float32

ROWS = 1536
HALF = ROWS // 2
QUAD = HALF // 2
SIDE = QUAD // 2
PART = SIDE // 2
FF_UNITS = 12
UNITS = 18
BLOCK = 256
GAIN_SPACING = 16


VMEM_LIMIT = 54 * 2 ** 20

SCHEDULE = (
    ((0, 0),),
    ((0, 1),),
    ((0, 2),),
    ((0, 3), (1, 0),),
    ((0, 4), (1, 1),),
    ((0, 5),),
    ((1, 3), (1, 2), (0, 7), (2, 0),),
    ((2, 1), (1, 4), (0, 9),),
    ((1, 5), (2, 3), (0, 11), (3, 0),),
    ((1, 7), (3, 1), (2, 2),),
    ((4, 0), (2, 5), (2, 4), (3, 3), (1, 11), (1, 9),),
    ((0, 6), (3, 2),),
    ((4, 1), (5, 0), (2, 7),),
    ((0, 8), (3, 5), (2, 11),),
    ((1, 6), (0, 10), (4, 3), (3, 4), (2, 9),),
    ((6, 0), (4, 2), (5, 1),),
    ((0, 12), (1, 8), (3, 7),),
    ((1, 10), (4, 5), (4, 4), (7, 0), (5, 3), (3, 11), (2, 6), (3, 9), (5, 2),),
    ((2, 8), (1, 12), (6, 1), (4, 7), (5, 5),),
    ((0, 13), (0, 14), (5, 4), (6, 2), (2, 10), (6, 3), (8, 0),),
    ((4, 11), (2, 12), (4, 9), (3, 6), (6, 5), (5, 7),),
    ((3, 8), (1, 13), (3, 10), (7, 2), (9, 0), (1, 14), (7, 1),),
    ((0, 15), (6, 4), (5, 11), (5, 9), (3, 12), (7, 3),),
    ((4, 6), (8, 2), (6, 7), (7, 5), (10, 0),),
    ((1, 15), (4, 8), (6, 9), (4, 10), (2, 13), (8, 1), (6, 11),),
    ((2, 14), (0, 16), (0, 17), (4, 12), (5, 6), (8, 3),),
    ((7, 4), (8, 5), (5, 8), (5, 10), (9, 2),),
    ((7, 7), (3, 13),),
    ((1, 16), (3, 14), (9, 1), (2, 15),),
    ((1, 17), (9, 3), (6, 6), (7, 9), (5, 12), (6, 8), (8, 4),),
    ((9, 5), (7, 11), (6, 10), (4, 13), (8, 7), (10, 2), (2, 16), (3, 15), (4, 14), (10, 1), (2, 17), (8, 9),
     (7, 6), (8, 11), (7, 8), (3, 16), (7, 10), (3, 17), (9, 4), (10, 3), (6, 12), (9, 7), (10, 5), (5, 13),
     (5, 14), (4, 15), (10, 4), (9, 9), (10, 7), (9, 11), (6, 13), (6, 14), (5, 15), (4, 16), (10, 9), (4, 17),
     (10, 11), (6, 15), (5, 16), (5, 17), (7, 12), (8, 6), (9, 6), (6, 16), (6, 17), (8, 8), (9, 8), (7, 13),
     (8, 10), (9, 10), (10, 6), (7, 14), (8, 12), (9, 12), (10, 8), (8, 13), (7, 15), (8, 14), (9, 13), (10, 10),
     (9, 14), (10, 12), (7, 16), (8, 15), (7, 17), (9, 15), (10, 13), (8, 16), (9, 16), (10, 14), (8, 17), (9, 17),
     (10, 15), (10, 16), (10, 17),),
)


def al(v, m):
    return pl.multiple_of(v, m)


class Ring:
    def __init__(self, grads, far, line, near, beyond, out, send_sem, recv_sem, own_sem, dp_size):
        self.grads, self.far, self.line, self.near, self.beyond, self.out = grads, far, line, near, beyond, out
        self.send_sem, self.recv_sem, self.own_sem = send_sem, recv_sem, own_sem
        self.extra = (dp_size // 16).bit_length() - 1
        self.dp = lax.axis_index("dp")
        self.mp = lax.axis_index("mp")
        place = lax.rem(lax.div(self.dp, 4), 4)
        low = jnp.where(place < 2, 1, 0)
        self.is_end = (place == 0) | (place == 3)
        self.is_mid = (place == 1) | (place == 2)
        self.inward = self.dp + 4 * (2 * low - 1)
        self.outward = self.dp - 4 * (2 * low - 1)
        self.far_side = low * SIDE
        self.own_side = (1 - low) * SIDE
        bits = (lax.rem(self.dp, 2), lax.rem(lax.div(self.dp, 2), 2))
        self.first_bit = bits
        self.last_bit = (bits[1], bits[0])
        self.first_peer = [self.dp + (1 - 2 * bits[h]) * (1 << h) for h in range(2)]
        self.last_peer = [self.first_peer[1], self.first_peer[0]]

    def kept(self, h, offset, count):
        return pl.ds(al(h * HALF + self.first_bit[h] * QUAD + offset, 16), count)

    def side(self, offset, count=SIDE):
        return pl.ds(al(offset, 16), count)

    def copy(self, src, dst, u, sent, received, dp):
        return pltpu.make_async_remote_copy(
            src_ref=src, dst_ref=dst, send_sem=self.send_sem.at[sent], recv_sem=self.recv_sem.at[u, received],
            device_id=(dp, self.mp), device_id_type=MESH)

    def received(self, block, u, k):
        self.copy(block, block, u, k, k, self.first_peer[0]).wait_recv()

    def was_sent(self, block, k):
        self.copy(block, block, 0, k, 0, self.first_peer[0]).wait_send()

    def add(self, u, rows, other):
        self.grads[u, rows] = (self.grads[u, rows].astype(f32) + other.astype(f32)).astype(bf16)

    def pass_sum(self, u, offset, sent, received, dp):
        for h in range(2):
            self.copy(self.grads.at[u, self.kept(h, offset, SIDE)], self.line.at[u, h, self.side(offset)],
                      u, sent, received, dp).start()

    def take_sum(self, u, offset, received):
        self.received(self.line.at[u, :, self.side(offset)], u, received)
        for h in range(2):
            self.add(u, self.kept(h, offset, SIDE), self.line[u, h, self.side(offset)])

    def pass_whole(self, u, offset, sent, received, dp):
        for h in range(2):
            block = self.far.at[u, h, self.side(offset)]
            self.copy(block, block, u, sent, received, dp).start()

    def take_whole(self, u, offset, received):
        self.received(self.far.at[u, :, self.side(offset)], u, received)

    def finish(self, u):
        for h in range(2):
            rows = self.kept(h, 0, QUAD)
            self.copy(self.far.at[u, h], self.out.at[u, rows], u, 5, 5, self.first_peer[h]).start()
            pltpu.make_async_copy(self.far.at[u, h], self.out.at[u, rows], self.own_sem.at[0]).start()

    def stage0(self, u):
        for h in range(2):
            rows = pl.ds(al(h * HALF + (1 - self.first_bit[h]) * QUAD, 16), QUAD)
            self.copy(self.grads.at[u, rows], self.far.at[u, h], u, 0, 0, self.first_peer[h]).start()

    def stage1(self, u):
        self.received(self.far.at[u], u, 0)
        for h in range(2):
            self.add(u, self.kept(h, 0, QUAD), self.far[u, h])

        @pl.when(self.is_end)
        def _():
            self.pass_sum(u, self.far_side, 1, 1, self.inward)

    def stage2(self, u):
        @pl.when(self.is_mid)
        def _():
            self.take_sum(u, self.far_side, 1)
            self.pass_sum(u, self.far_side, 1, 2, self.inward)

    def stage3(self, u):
        @pl.when(self.is_mid)
        def _():
            self.take_sum(u, self.own_side, 2)
            self.pass_sum(u, self.own_side, 2, 2, self.outward)

    def stage4(self, u):
        @pl.when(self.is_end)
        def _():
            self.take_sum(u, self.own_side, 2)
            for h in range(2):
                rows = self.kept(h, self.own_side + (1 - self.last_bit[h]) * PART, PART)
                self.copy(self.grads.at[u, rows], self.near.at[u, h], u, 2, 1, self.last_peer[h]).start()

    def stage5(self, u):
        @pl.when(self.is_end)
        def _():
            self.received(self.near.at[u], u, 1)
            for h in range(2):
                offset = self.own_side + self.last_bit[h] * PART
                mine = self.kept(h, offset, PART)
                last = self.near[u, h]
                for k in range(self.extra):
                    self.add(u, mine, last)
                    copy = self.copy(self.grads.at[u, mine], self.beyond.at[u, h, k], u, 6 + 2 * k + h, 6 + 2 * k + h,
                                     self.dp ^ (16 << k))
                    copy.start()
                    copy.wait()
                    last = self.beyond[u, h, k]
                rows = self.side(offset, PART)
                self.far[u, h, rows] = (self.grads[u, mine].astype(f32) + last.astype(f32)).astype(bf16)
                block = self.far.at[u, h, rows]
                self.copy(block, block, u, 3, 3, self.last_peer[h]).start()

    def stage6(self, u):
        @pl.when(self.is_end)
        def _():
            self.received(self.near.at[u], u, 3)
            self.pass_whole(u, self.own_side, 4, 3, self.inward)

    def stage7(self, u):
        @pl.when(self.is_mid)
        def _():
            self.take_whole(u, self.own_side, 3)
            self.pass_whole(u, self.own_side, 3, 4, self.inward)

    def stage8(self, u):
        @pl.when(self.is_mid)
        def _():
            self.take_whole(u, self.far_side, 4)
            self.pass_whole(u, self.far_side, 4, 4, self.outward)
            self.finish(u)

    def stage9(self, u):
        @pl.when(self.is_end)
        def _():
            self.take_whole(u, self.far_side, 4)
            self.finish(u)

    def stage10(self, u):
        self.received(self.far.at[u], u, 5)

    def sent(self):
        self.was_sent(self.far, 0)
        self.was_sent(self.far, 5)
        pltpu.make_async_copy(self.far, self.far, self.own_sem.at[0]).wait()
        one_side = self.line.at[:, :, pl.ds(0, SIDE)]

        @pl.when(self.is_end)
        def _():
            for k, block in ((1, one_side), (2, self.near), (3, self.near), (4, one_side)):
                self.was_sent(block, k)

        @pl.when(self.is_mid)
        def _():
            for k in range(1, 5):
                self.was_sent(one_side, k)

    def stages(self):
        return (self.stage0, self.stage1, self.stage2, self.stage3, self.stage4, self.stage5, self.stage6,
                self.stage7, self.stage8, self.stage9, self.stage10)


def dot(a, b):
    return jnp.dot(a, b, preferred_element_type=f32)


def dot_nt(a, b):
    return lax.dot_general(a, b, (((1,), (1,)), ((), ())), preferred_element_type=f32)


def normalize(values):
    centred = values - jnp.mean(values, axis=-1, keepdims=True)
    inv_std = lax.rsqrt(jnp.mean(centred * centred, axis=-1, keepdims=True) + EPSILON)
    return centred * inv_std, inv_std


def norm_back(grad, scaled, inv_std, gain):
    grad_scaled = grad * gain
    mean_first = jnp.mean(grad_scaled, axis=-1, keepdims=True)
    mean_second = jnp.mean(grad_scaled * scaled, axis=-1, keepdims=True)
    return inv_std * (grad_scaled - mean_first - scaled * mean_second), jnp.sum(grad * scaled, axis=0, keepdims=True)


def layer_kernel(
    dp_size, mol_hbm, gain_one_hbm, wq_hbm, wk_hbm, wv_hbm, wo_hbm, gain_two_hbm, wi_hbm, wu_hbm, cot_hbm, mask_hbm,
    act_out, gmol_out, sums_out, gains_out,
    gains, mask_ref, x, cot, wqkv, wo, wi, wu, n1, turned, qkv, mixed, mixed_t, pin, pout, n2, gres, act, gip, lse, hid,
    gains_sum, gains_in, grads, far, line, near, beyond,
    in_sem, mp_send, mp_recv, gain_send, gain_recv, ring_send, ring_recv, ring_own,
):
    mp = lax.axis_index("mp")
    dp = lax.axis_index("dp")
    rows, width = n1.shape
    half = rows // 2
    shard = half // 2
    heads_width = wo.shape[0]
    pairs = heads_width // 128
    joined = 3 * 128
    ring = Ring(grads, far, line, near, beyond, sums_out, ring_send, ring_recv, ring_own, dp_size)
    stages = ring.stages()
    own = pl.ds(al(mp * half, half), half)
    other = pl.ds(al((1 - mp) * half, half), half)
    gbr = n2
    slot = iter(SCHEDULE)

    def advance():
        for stage, unit in next(slot, ()):
            stages[stage](unit)

    def own_of(s):
        return pl.ds(al(mp * half + s * shard, shard), shard)

    def other_of(s):
        return pl.ds(al((1 - mp) * half + s * shard, shard), shard)

    def take(ref, s, columns):
        return jnp.concatenate([ref[pl.ds(s * shard, shard), columns], ref[pl.ds(half + s * shard, shard), columns]])

    def put(ref, s, columns, values):
        ref[pl.ds(s * shard, shard), columns] = values[:shard]
        ref[pl.ds(half + s * shard, shard), columns] = values[shard:]

    def to_peer(src, dst, k):
        return pltpu.make_async_remote_copy(
            src_ref=src, dst_ref=dst, send_sem=mp_send.at[k], recv_sem=mp_recv.at[k],
            device_id=(dp, 1 - mp), device_id_type=MESH)

    def rows_copy(ref, s, k):
        return to_peer(ref.at[own_of(s)], ref.at[own_of(s)], k)

    def part_copy(kind, s):
        return to_peer(pout.at[kind % 2, s], pin.at[kind % 3, s], 8 + 2 * kind + s)

    def whole_part(kind):
        return to_peer(pout.at[kind % 2], pin.at[kind % 3], 8 + 2 * kind)

    gain_one = gains.at[pl.ds(0, 1)]
    gain_two = gains.at[pl.ds(1, 1)]

    loads = [
        pltpu.make_async_copy(mol_hbm.at[0], x.at[0], in_sem.at[0]),
        pltpu.make_async_copy(mol_hbm.at[1], x.at[1], in_sem.at[1]),
    ]
    for kind, source in enumerate((wq_hbm, wk_hbm, wv_hbm)):
        for pair in range(pairs):
            loads.append(pltpu.make_async_copy(
                source.at[:, pl.ds(pair * 128, 128)], wqkv.at[:, pl.ds(pair * joined + kind * 128, 128)],
                in_sem.at[len(loads)]))
    weights = loads[2:]
    others = []
    for source, target in ((cot_hbm, cot), (wo_hbm, wo), (wi_hbm, wi), (wu_hbm, wu)):
        others.append(pltpu.make_async_copy(source, target, in_sem.at[len(loads) + len(others)]))
    gain_loads = [
        pltpu.make_async_copy(source, gains.at[k], in_sem.at[len(loads) + len(others) + k])
        for k, source in enumerate((gain_one_hbm, gain_two_hbm))
    ]
    mask_load = pltpu.make_async_copy(mask_hbm, mask_ref, in_sem.at[len(loads) + len(others) + 2])
    for load in gain_loads + loads + [mask_load] + others:
        load.start()

    barrier = pltpu.get_barrier_semaphore()
    flips = [1, 2, 4, 8, 12] + [16 << k for k in range(ring.extra)]
    for flip in flips:
        pl.semaphore_signal(barrier, inc=1, device_id=(dp ^ flip, mp), device_id_type=MESH)
    pl.semaphore_signal(barrier, inc=1, device_id=(dp, 1 - mp), device_id_type=MESH)

    for load in gain_loads:
        load.wait()
    for s in range(2):
        loads[s].wait()
        scaled, _ = normalize(x[s].astype(f32))
        n1[own_of(s), :] = (scaled * gain_one[...]).astype(bf16)
        if s == 0:
            pl.semaphore_wait(barrier, len(flips) + 1)
        rows_copy(n1, s, s).start()

    mask_load.wait()
    others[0].wait()
    lanes = lax.broadcasted_iota(jnp.int32, (128, 128), 1)
    subs = lax.broadcasted_iota(jnp.int32, (128, 128), 0)
    for s in range(2):
        for piece in range(shard // 128):
            row = mask_ref[pl.ds(s, 1), pl.ds(piece * 128, 128)].astype(f32)
            column = jnp.sum(jnp.where(lanes == subs, row, 0.0), axis=1, keepdims=True)
            weight = 0.25 + 0.75 * column
            values = cot[s, pl.ds(piece * 128, 128), :].astype(f32) * weight
            gres[pl.ds(al(mp * half + s * shard + piece * 128, 128), 128), :] = values.astype(bf16)
        rows_copy(gres, s, 2 + s).start()

    lane = lax.broadcasted_iota(jnp.int32, (1, 128), 1)
    sides = (lane < HEAD_DIM, lane >= HEAD_DIM)
    scale = HEAD_DIM ** -0.5

    def columns(pair, kind):
        return pl.ds(pair * joined + kind * 128, 128)

    for load in weights:
        load.wait()
    qkv[own, :] = dot(n1[own, :], wqkv[...]).astype(bf16)
    for s in range(2):
        rows_copy(n1, s, s).wait_recv()
    qkv[other, :] = dot(n1[other, :], wqkv[...]).astype(bf16)
    others[1].wait()

    def second_norm(s):
        part_copy(0, s).wait_recv()
        hidden = hid[s] + pin[0, s].astype(f32)
        hid[s] = hidden
        scaled, _ = normalize(hidden)
        n2[own_of(s), :] = (scaled * gain_two[...]).astype(bf16)
        rows_copy(n2, s, 4 + s).start()

    for s in range(2):
        logs = jnp.zeros((half, 128), f32)
        for pair in range(pairs):
            query = take(qkv, s, columns(pair, 0)) * jnp.asarray(scale, bf16)
            key = take(qkv, s, columns(pair, 1))
            value = take(qkv, s, columns(pair, 2))
            outs = []
            for side in range(2):
                scores = dot_nt(jnp.where(sides[side], query, 0), key)
                row_max = jnp.max(scores, axis=-1, keepdims=True)
                expon = jnp.exp(scores - row_max)
                total = jnp.sum(expon, axis=-1, keepdims=True)
                logs = jnp.where(lane == 2 * pair + side, row_max + jnp.log(total), logs)
                outs.append(dot(expon.astype(bf16), value) * (1.0 / total))
            put(mixed, s, pl.ds(pair * 128, 128), jnp.where(sides[0], outs[0], outs[1]).astype(bf16))
            if s == 1 and pair == 1:
                second_norm(0)
        lse[s] = logs
        pout[0, s] = dot(mixed[other_of(s), :], wo[...]).astype(bf16)
        part_copy(0, s).start()
        hid[s] = x[s].astype(f32) + dot(mixed[own_of(s), :], wo[...])
    second_norm(1)
    mixed_t[...] = mixed[...].T
    turned[:, own] = n2[own, :].T
    for s in range(2):
        rows_copy(gres, s, 2 + s).wait_recv()
    others[2].wait()
    others[3].wait()
    for s in range(2):
        rows_copy(n2, s, 4 + s).wait_recv()
    turned[:, other] = n2[other, :].T

    def grad_outer(b):
        part = dot(act[:, pl.ds(b * BLOCK, BLOCK)].T, gres[...]).astype(bf16)
        for g in range(width // 128):
            grads[2 * b, pl.ds(g * BLOCK, BLOCK), :] = part[:, g * 128:(g + 1) * 128]
        advance()

    blocks = wi.shape[1] // BLOCK
    for b in range(blocks):
        block = pl.ds(b * BLOCK, BLOCK)
        inner = dot(n2[...], wi[:, block])
        shape = 1.0 + lax.erf(inner * (0.5 ** 0.5))
        act[:, block] = (0.5 * inner * shape).astype(bf16)
        slope = 0.5 * shape + inner * (jnp.exp(-0.5 * inner * inner) * (2.0 * 3.141592653589793) ** -0.5)
        if b < blocks // 2:
            grad_outer(b)
        back = dot_nt(gres[...], wu[block, :])
        pre = (back * slope).astype(bf16)
        gip[:, block] = pre
        part = dot(turned[...], pre).astype(bf16)
        for g in range(BLOCK // 128):
            grads[2 * b + 1, pl.ds(g * width, width), :] = part[:, g * 128:(g + 1) * 128]
        advance()

    def send_part(kind, values):
        if kind >= 2:
            for s in range(2 if kind == 2 else 0):
                part_copy(0, s).wait_send()
            if kind == 3:
                whole_part(1).wait_send()
        for s in range(2):
            pout[kind % 2, s] = values[s * shard:(s + 1) * shard].astype(bf16)
        whole_part(kind).start()

    send_part(1, dot_nt(gip[other, :], wi[...]))
    advance()
    grad = dot_nt(gip[own, :], wi[...])
    turned[...] = n1[...].T
    advance()
    grad_outer(blocks // 2)
    whole_part(1).wait_recv()
    gain_two_sum = jnp.zeros((1, width), f32)
    for s in range(2):
        scaled, inv_std = normalize(hid[s])
        grad_values, gain_part = norm_back(
            grad[s * shard:(s + 1) * shard] + pin[1, s].astype(f32), scaled, inv_std, gain_two[...])
        gain_two_sum += gain_part
        grad_hidden = gres[own_of(s), :].astype(f32) + grad_values
        gbr_rows = grad_hidden.astype(bf16)
        if s == 0:
            for k in range(2):
                rows_copy(n2, k, 4 + k).wait_send()
        gmol_out[s] = grad_hidden
        gbr[own_of(s), :] = gbr_rows
        rows_copy(gbr, s, 6 + s).start()
    advance()
    for b in range(blocks // 2 + 1, blocks):
        grad_outer(b)
    for s in range(2):
        rows_copy(gbr, s, 6 + s).wait_recv()
    mixed[...] = dot_nt(gbr[...], wo[...]).astype(bf16)
    advance()
    part = dot(mixed_t[...], gbr[...]).astype(bf16)
    for g in range(width // 128):
        at = g * heads_width
        grads[FF_UNITS + at // ROWS, pl.ds(at % ROWS, heads_width), :] = part[:, g * 128:(g + 1) * 128]
    advance()

    for pair in range(pairs):
        for s in range(2):
            query = take(qkv, s, columns(pair, 0)) * jnp.asarray(scale, bf16)
            key = take(qkv, s, columns(pair, 1))
            value = take(qkv, s, columns(pair, 2))
            grad_mixed = take(mixed, s, pl.ds(pair * 128, 128))
            logs = lse[s]
            query_t = query.T
            grad_mixed_t = grad_mixed.T
            found = []
            for side in range(2):
                log_total = jnp.sum(jnp.where(lane == 2 * pair + side, logs, 0.0), axis=-1, keepdims=True)
                probs = jnp.exp(dot_nt(jnp.where(sides[side], query, 0), key) - log_total)
                grad_probs = dot_nt(jnp.where(sides[side], grad_mixed, 0), value)
                row_inner = jnp.sum(probs * grad_probs, axis=-1, keepdims=True)
                grad_scores = (probs * (grad_probs - row_inner)).astype(bf16)
                grad_value = dot(grad_mixed_t, probs.astype(bf16))
                grad_query = dot(grad_scores, key) * scale
                grad_key = dot(query_t, grad_scores)
                found.append((grad_query, grad_key, grad_value))
            put(gip, s, columns(pair, 0), jnp.where(sides[0], found[0][0], found[1][0]).astype(bf16))
            for kind in (1, 2):
                joint = jnp.concatenate([found[0][kind][:HEAD_DIM], found[1][kind][HEAD_DIM:]])
                put(gip, s, columns(pair, kind), joint.astype(bf16).T)
            advance()
        part = dot(turned[...], gip[:, pl.ds(pair * joined, joined)]).astype(bf16)
        for kind in range(3):
            at = width // 128 * heads_width + (pair * 3 + kind) * width
            grads[FF_UNITS + at // ROWS, pl.ds(at % ROWS, width), :] = part[:, kind * 128:(kind + 1) * 128]
        advance()

    all_joined = pl.ds(0, pairs * joined)
    send_part(3, dot_nt(gip[other, all_joined], wqkv[...]))
    advance()
    grad = dot_nt(gip[own, all_joined], wqkv[...])
    advance()
    send_part(2, dot(act[other, :], wu[...]))
    advance()
    result = dot(act[own, :], wu[...])
    whole_part(2).wait_recv()
    for s in range(2):
        act_out[s] = (hid[s] + result[s * shard:(s + 1) * shard] + pin[2, s].astype(f32)).astype(bf16)
    advance()
    whole_part(3).wait_recv()
    gain_one_sum = jnp.zeros((1, width), f32)
    for s in range(2):
        scaled, inv_std = normalize(x[s].astype(f32))
        grad_values, gain_part = norm_back(
            grad[s * shard:(s + 1) * shard] + pin[0, s].astype(f32), scaled, inv_std, gain_one[...])
        gain_one_sum += gain_part
        gmol_out[s] = gmol_out[s] + grad_values
    gains_sum[0] = jnp.zeros(gains_sum.shape[1:], f32)
    gains_sum[0, pl.ds(0, 1), :] = gain_one_sum
    gains_sum[0, pl.ds(1, 1), :] = gain_two_sum

    targets = [(dp, 1 - mp)] + [(dp ^ (1 << k), mp) for k in range(4 + ring.extra)]

    def gain_copy(k):
        return pltpu.make_async_remote_copy(
            src_ref=gains_sum.at[k], dst_ref=gains_in.at[k], send_sem=gain_send.at[k], recv_sem=gain_recv.at[k],
            device_id=targets[k], device_id_type=MESH)

    def gain_step(k):
        if k:
            gain_copy(k - 1).wait_recv()
            total = gains_sum[k - 1] + gains_in[k - 1]
            if k == len(targets):
                gains_out[...] = total
            else:
                gains_sum[k] = total
        if k < len(targets):
            gain_copy(k).start()

    tail = [step for part in slot for step in part]
    steps = len(targets) + 1
    for i, (stage, unit) in enumerate(tail):
        if i % GAIN_SPACING == 0 and i // GAIN_SPACING < steps:
            gain_step(i // GAIN_SPACING)
        stages[stage](unit)
    for k in range(-(-len(tail) // GAIN_SPACING), steps):
        gain_step(k)

    for s in range(2):
        rows_copy(n1, s, s).wait_send()
        rows_copy(gres, s, 2 + s).wait_send()
        rows_copy(gbr, s, 6 + s).wait_send()
    for kind in (2, 3):
        whole_part(kind).wait_send()
    for k in range(len(targets)):
        gain_copy(k).wait_send()
    ring.sent()


def finish_kernel(
    act_in, gmol_in, packed, gains_in, act_out, gmol_out, gq, gk, gv, go, gi, gu, gain_one_out, gain_two_out,
    query, key, value, output, inner, outer, out_sem,
):
    width, heads_width = query.shape
    outs = []

    def send(src, dst):
        copy = pltpu.make_async_copy(src, dst, out_sem.at[len(outs)])
        copy.start()
        outs.append(copy)
    send(act_in, act_out)
    send(gmol_in, gmol_out)
    send(gains_in.at[0], gain_one_out)
    send(gains_in.at[1], gain_two_out)
    for b in range(FF_UNITS // 2):
        for g in range(width // 128):
            outer[pl.ds(b * BLOCK, BLOCK), pl.ds(g * 128, 128)] = packed[2 * b, pl.ds(g * BLOCK, BLOCK), :].astype(f32)
        send(outer.at[pl.ds(b * BLOCK, BLOCK)], gu.at[pl.ds(b * BLOCK, BLOCK)])
        for g in range(BLOCK // 128):
            inner[:, pl.ds(b * BLOCK + g * 128, 128)] = packed[2 * b + 1, pl.ds(g * width, width), :].astype(f32)
        send(inner.at[:, pl.ds(b * BLOCK, BLOCK)], gi.at[:, pl.ds(b * BLOCK, BLOCK)])
    at = FF_UNITS * ROWS

    def unpack(block, g, at):
        count = block.shape[0]
        block[:, pl.ds(g * 128, 128)] = packed[at // ROWS, pl.ds(at % ROWS, count), :].astype(f32)
        return at + count
    for g in range(width // 128):
        at = unpack(output, g, at)
    send(output, go)
    for pair in range(heads_width // 128):
        for block in (query, key, value):
            at = unpack(block, pair, at)
    for block, target in ((query, gq), (key, gk), (value, gv)):
        send(block, target)
    for copy in outs:
        copy.wait()


ANY = pl.BlockSpec(memory_space=pl.ANY)
WHOLE = pl.BlockSpec(memory_space=pltpu.VMEM)


def per_device(
    dp_size, molecules, gain_attn, w_query, w_key, w_value, w_output, gain_ffn, w_inner, w_outer, cotangent, span_mask
):
    count, shard, width = molecules.shape
    heads_width = w_query.shape[1]
    units_inner = w_inner.shape[1]
    rows = 2 * count * shard
    extra = (dp_size // 16).bit_length() - 1
    levels = 5 + extra
    act, gmol, sums, gains = pl.pallas_call(
        functools.partial(layer_kernel, dp_size),
        out_shape=(
            pltpu.VMEM(molecules.shape, bf16),
            pltpu.VMEM(molecules.shape, f32),
            pltpu.VMEM((UNITS, ROWS, 128), bf16),
            pltpu.VMEM((8, width), f32),
        ),
        in_specs=[ANY] * 11,
        out_specs=(WHOLE, WHOLE, WHOLE, WHOLE),
        scratch_shapes=[
            pltpu.VMEM((8, width), f32),
            pltpu.VMEM(span_mask.shape, jnp.int32),
            pltpu.VMEM(molecules.shape, bf16),
            pltpu.VMEM(molecules.shape, bf16),
            pltpu.VMEM((width, 3 * heads_width), bf16),
            pltpu.VMEM(w_output.shape, bf16),
            pltpu.VMEM(w_inner.shape, bf16),
            pltpu.VMEM(w_outer.shape, bf16),
            pltpu.VMEM((rows, width), bf16),
            pltpu.VMEM((width, rows), bf16),
            pltpu.VMEM((rows, 3 * heads_width), bf16),
            pltpu.VMEM((rows, heads_width), bf16),
            pltpu.VMEM((heads_width, rows), bf16),
            pltpu.VMEM((3,) + molecules.shape, bf16),
            pltpu.VMEM((2,) + molecules.shape, bf16),
            pltpu.VMEM((rows, width), bf16),
            pltpu.VMEM((rows, width), bf16),
            pltpu.VMEM((rows, units_inner), bf16),
            pltpu.VMEM((rows, units_inner), bf16),
            pltpu.VMEM((count, rows // 2, 128), f32),
            pltpu.VMEM(molecules.shape, f32),
            pltpu.VMEM((levels, 8, width), f32),
            pltpu.VMEM((levels, 8, width), f32),
            pltpu.VMEM((UNITS, ROWS, 128), bf16),
            pltpu.VMEM((UNITS, 2, QUAD, 128), bf16),
            pltpu.VMEM((UNITS, 2, QUAD, 128), bf16),
            pltpu.VMEM((UNITS, 2, PART, 128), bf16),
            pltpu.VMEM((UNITS if extra else 1, 2, max(extra, 1), PART, 128), bf16),
            pltpu.SemaphoreType.DMA((18,)),
            pltpu.SemaphoreType.DMA((16,)),
            pltpu.SemaphoreType.DMA((16,)),
            pltpu.SemaphoreType.DMA((levels,)),
            pltpu.SemaphoreType.DMA((levels,)),
            pltpu.SemaphoreType.DMA((6 + 2 * extra,)),
            pltpu.SemaphoreType.DMA((UNITS, 6 + 2 * extra)),
            pltpu.SemaphoreType.DMA((1,)),
        ],
        compiler_params=pltpu.CompilerParams(
            collective_id=0, has_side_effects=True, vmem_limit_bytes=VMEM_LIMIT),
        name="layer",
    )(
        molecules, gain_attn, w_query, w_key, w_value, w_output, gain_ffn,
        w_inner, w_outer, cotangent, span_mask,
    )
    shapes = [jax.ShapeDtypeStruct(w.shape, f32) for w in (w_query, w_key, w_value, w_output, w_inner, w_outer)]
    outs = pl.pallas_call(
        finish_kernel,
        out_shape=(
            jax.ShapeDtypeStruct(molecules.shape, bf16), jax.ShapeDtypeStruct(molecules.shape, f32), *shapes,
            jax.ShapeDtypeStruct((width,), f32), jax.ShapeDtypeStruct((width,), f32)),
        in_specs=[WHOLE] * 4,
        out_specs=(ANY,) * 10,
        scratch_shapes=[pltpu.VMEM(shape.shape, f32) for shape in shapes]
        + [pltpu.SemaphoreType.DMA((4 + FF_UNITS + 4,))],
        compiler_params=pltpu.CompilerParams(vmem_limit_bytes=40 * 2 ** 20),
        name="finish",
    )(act, gmol, sums, gains)
    return tuple(outs)


def solution(mesh):
    in_specs = (
        P("dp", "mp", None),
        P(),
        P(None, "mp"),
        P(None, "mp"),
        P(None, "mp"),
        P("mp", None),
        P(),
        P(None, "mp"),
        P("mp", None),
        P("dp", "mp", None),
        P("dp", "mp"),
    )
    out_specs = (
        P("dp", "mp", None),
        P("dp", "mp", None),
        P(None, "mp"),
        P(None, "mp"),
        P(None, "mp"),
        P("mp", None),
        P(None, "mp"),
        P("mp", None),
        P(),
        P(),
    )
    return jax.shard_map(
        functools.partial(per_device, mesh.shape["dp"]),
        mesh=mesh, in_specs=in_specs, out_specs=out_specs, check_vma=False,
    )
```
